128 devices in a mesh: row: 16 (over z_lo, x, core), col: 8 (over y, z_hi).
Axes of the slice: x: 4, y: 4, z: 4 (z_hi: 2, z_lo: 2; z = z_hi * 2 + z_lo), core: 2. Of those that a mesh axis runs over, the one named last changes fastest.
Arguments:
- tile_u: float32 [16, 32, 2048, 128], P('row', 'col'), may hold values from -6 to 6
- tile_v: float32 [16, 32, 2048, 128], P('row', 'col'), may hold values from -1.5 to 1.5
- row_panel_u: float32 [16, 2048, 128], P('row', 'col'), may hold values from -6 to 6
- row_panel_v: float32 [16, 2048, 128], P('row', 'col'), may hold values from -0.125 to 0.125
- col_panel_u: float32 [32, 2048, 128], P('row', 'col'), may hold values from -6 to 6
- col_panel_v: float32 [32, 2048, 128], P('row', 'col'), may hold values from -0.125 to 0.125
- diag_inverse: float32 [2048, 2048], P('col'), may hold values from -0.15 to 2, as said below
- sketch: float32 [2048, 128], replicated, may hold values from -0.125 to 0.125
Outputs:
- new_u: float32 [16, 32, 2048, 128], P('row', 'col')
- new_v: float32 [16, 32, 2048, 128], P('row', 'col')
The draws below stay inside these ranges and needn't reach their ends.
Inputs may be any that keep to these rules, and one draw needn't show every extreme that they name: `diag_inverse`: lower triangular; the diagonal lies between 0.5 and 2, the entries below it between -0.15 and 0.15.
All inputs are finite; a program needn't handle non-finite values.
Results may differ from the reference program's by a relative error of at most 0.0003.
Values sent between devices are 32-bit elements; how exact they have to be, the bound alone decides.
A program may use at most 128 MiB of HBM per device.

```python
import math
import jax
import jax.numpy as jnp
from jax import lax

B = 2048
K = 128
RT = 16
CT = 32


def draw_diag_inverse(key, part):
    first_key, second_key = jax.random.split(jax.random.fold_in(key, 17))
    diagonal = jax.random.uniform(first_key, (B,), jnp.float32, 0.5, 2.0)
    strict = jax.random.normal(second_key, (B, B), jnp.float32) / math.sqrt(B)
    strict = jnp.clip(strict, -0.15, 0.15)
    return jnp.tril(strict, -1) + jnp.diag(diagonal)


def block_scale(own_key, extent, pieces, low, largest):
    level, own = 1.0, jax.random.fold_in(own_key, 6)
    for axis_at, parts in pieces:
        steps = jnp.exp(jax.random.uniform(jax.random.fold_in(own, axis_at), (parts,), jnp.float32, low / len(pieces), largest / len(pieces)))
        level = level * jnp.repeat(steps, extent[axis_at] // parts).reshape([-1 if axis == axis_at else 1 for axis in range(len(extent))])
    return level


def scatter_about(stream_key, dims, deviation, bound, shards=(), dtype=jnp.bfloat16):
    result = jax.random.normal(stream_key, dims, jnp.float32) * deviation
    if len(shards) > 0:
        result = block_scale(stream_key, dims, shards, -0.22, 0.18) * result
    return jnp.clip(result, min=-bound, max=bound).astype(dtype)


def setup_inputs(seed: int = 0) -> dict:
    splits = jax.random.split(jax.random.key(seed), 9)
    return {
        "tile_u": scatter_about(splits[0], (RT, CT, B, K), 1.0, 6.0, ((0, 16), (1, 8)), jnp.float32),
        "tile_v": scatter_about(splits[1], (RT, CT, B, K), 0.25, 1.5, ((0, 16), (1, 8)), jnp.float32),
        "row_panel_u": scatter_about(splits[2], (RT, B, K), 1.0, 6.0, ((0, 16), (1, 8)), jnp.float32),
        "row_panel_v": scatter_about(splits[3], (RT, B, K), B ** -0.5, 0.125, ((0, 16), (1, 8)), jnp.float32),
        "col_panel_u": scatter_about(splits[4], (CT, B, K), 1.0, 6.0, ((0, 16), (1, 8)), jnp.float32),
        "col_panel_v": scatter_about(splits[5], (CT, B, K), B ** -0.5, 0.125, ((0, 16), (1, 8)), jnp.float32),
        "diag_inverse": draw_diag_inverse(jax.random.fold_in(splits[8], 71), 0),
        "sketch": scatter_about(splits[7], (B, K), B ** -0.5, 0.125, (), jnp.float32),
    }


highest = lax.Precision.HIGHEST

def recompress(tile_u, tile_v, row_u, cores, col_u, sketch):
    branch = -jnp.einsum('iak,ijkl->ijal', row_u, cores, precision=highest)
    left_side = jnp.concatenate([tile_u, branch], axis=-1)
    right_side = jnp.concatenate([tile_v, jnp.broadcast_to(col_u[None], tile_v.shape)], axis=-1)
    projected = jnp.einsum('ijar,ak->ijrk', right_side, sketch, precision=highest)
    sample = jnp.einsum('ijar,ijrk->ijak', left_side, projected, precision=highest)
    gram_matrix = jnp.einsum('ijak,ijal->ijkl', sample, sample, precision=highest)
    factor = jnp.linalg.cholesky(gram_matrix)
    solved_t = jax.scipy.linalg.solve_triangular(factor, jnp.swapaxes(sample, -1, -2), lower=True)
    basis = jnp.swapaxes(solved_t, -1, -2)
    coefficients = jnp.einsum('ijar,ijak->ijrk', left_side, basis, precision=highest)
    scaling = math.sqrt(tile_u.shape[2])
    new_v = jnp.einsum('ijar,ijrk->ijak', right_side, coefficients, precision=highest) / scaling
    return (basis * scaling, new_v)

def reference(tile_u, tile_v, row_panel_u, row_panel_v, col_panel_u, col_panel_v, diag_inverse, sketch):
    row_solved = jnp.einsum('ab,tbk->tak', diag_inverse, row_panel_v, precision=highest)
    col_solved = jnp.einsum('ab,tbk->tak', diag_inverse, col_panel_v, precision=highest)

    def one_row(entries):
        row_tiles_u, row_tiles_v, panel_u, panel_v = entries
        cores = jnp.einsum('ak,jal->jkl', panel_v, col_solved, precision=highest)
        result_u, result_v = recompress(row_tiles_u[None], row_tiles_v[None], panel_u[None], cores[None], col_panel_u, sketch)
        return (result_u[0], result_v[0])
    new_u, new_v = lax.map(one_row, (tile_u, tile_v, row_panel_u, row_solved))
    return (new_u, new_v)
```

```python
import math

import jax
import jax.numpy as jnp
from jax import lax
from jax.experimental import pallas as pl
from jax.experimental.pallas import tpu as pltpu
from jax.sharding import PartitionSpec as P

highest = lax.Precision.HIGHEST
f32, bf16 = jnp.float32, jnp.bfloat16


def halves(x):
    hi = x.astype(bf16)
    lo = (x - hi.astype(f32)).astype(bf16)
    return jnp.concatenate([hi, lo], axis=1)


def fold4(q):
    k = q.shape[0] // 2
    n = q.shape[1] // 2
    return q[:k, :n] + q[:k, n:] + q[k:, :n] + q[k:, n:]


def doubled(w):
    h = halves(w)
    return jnp.concatenate([h, h], axis=0)


def dot(a, b, ca=1, cb=0, precision=highest):
    return lax.dot_general(a, b, (((ca,), (cb,)), ((), ())), precision=precision, preferred_element_type=f32)


def dotb(a, b, ca=1, cb=0):
    return lax.dot_general(a, b, (((ca,), (cb,)), ((), ())), preferred_element_type=f32)


def inverse_factors(gram_ref, inv_ref, fac_ref):
    tiles, k, _ = gram_ref.shape
    row = lax.broadcasted_iota(jnp.int32, (tiles, 8, k), 1)
    lane = lax.broadcasted_iota(jnp.int32, (tiles, 8, k), 2)
    for p in range(k // 8):
        lo = 8 * p
        panel = gram_ref[:, lo : lo + 8, :]
        if p == 0:
            own = jnp.zeros((tiles, 8, k), f32)
        else:
            own = inv_ref[:, lo : lo + 8, :]
        own = own + jnp.where(lane == row + lo, 1.0, 0.0)
        cols = [jnp.broadcast_to(panel[:, :, lo + i : lo + i + 1], panel.shape) for i in range(8)]
        scale = jnp.zeros((tiles, 8, k), f32)
        pivot = jnp.zeros((tiles, 8, k), f32)
        for i in range(8):
            piv = jnp.broadcast_to(cols[i][:, i : i + 1, :], panel.shape)
            recip = 1.0 / piv
            scale = jnp.where(row == i, recip, scale)
            if i < 7:
                m = jnp.where(row > i, cols[i] * recip, 0.0)
                for j in range(i + 1, 8):
                    cols[j] = cols[j] - m * cols[j][:, i : i + 1, :]
                panel = panel - m * panel[:, i : i + 1, :]
                own = own - m * own[:, i : i + 1, :]
        fac_ref[:, lo : lo + 8, :] = own * jnp.sqrt(scale)
        if p < k // 8 - 1:
            lower = panel * scale
            for t in range(tiles):
                both = jnp.concatenate([panel[t], own[t]], axis=1)
                upd = dot(lower[t], both, 0, 0)
                gram_ref[t, lo + 8 :, :] = gram_ref[t, lo + 8 :, :] - upd[lo + 8 :, :k]
                if p == 0:
                    inv_ref[t, lo + 8 :, :] = -upd[lo + 8 :, k:]
                else:
                    inv_ref[t, lo + 8 :, :] = inv_ref[t, lo + 8 :, :] - upd[lo + 8 :, k:]


def local_kernel(u_hbm, v_hbm, r_ref, c_hbm, cores_ref, s_ref, nu_hbm, nv_hbm,
                 ubuf, vbuf, cbuf, usp, vsp, csp, rsp, tt, w_s, t_s, gram_s, inv_s, fac_s, in_sem, out_sem):
    tiles, rows, k = ubuf.shape
    step = min(512, rows)
    scaling = math.sqrt(rows)

    def load(t, which):
        src, dst = ((u_hbm, ubuf), (v_hbm, vbuf), (c_hbm, cbuf))[which]
        return pltpu.make_async_copy(src.at[t], dst.at[t], in_sem.at[which, t])

    for t in range(tiles):
        for which in range(3):
            load(t, which).start()

    for lo in range(0, rows, step):
        for n, ref in enumerate((r_ref, s_ref)):
            h = halves(ref[lo : lo + step, :])
            if n == 0:
                rsp[lo : lo + step, :] = h
            tt[n, :, lo : lo + step] = h.astype(f32).T.astype(bf16)
    rr = fold4(dotb(tt[0], rsp[...]))

    for t in range(tiles):
        for which in range(3):
            load(t, which).wait()
            buf, sp = ((ubuf, usp), (vbuf, vsp), (cbuf, csp))[which]

            def body(n, carry, buf=buf, sp=sp, t=t):
                at = pl.ds(pl.multiple_of(n * step, step), step)
                sp[t, at, :] = halves(buf[t, at, :])
                return carry

            lax.fori_loop(0, rows // step, body, 0)
        uu = fold4(dotb(usp[t], usp[t], 0, 0))
        ru = fold4(dotb(tt[0], usp[t]))
        p1t = fold4(dotb(tt[1], vsp[t]))
        p2t = fold4(dotb(tt[1], csp[t]))
        cores = cores_ref[t]
        w1 = p1t.T
        w2 = -dot(cores, p2t, 1, 1)
        w = jnp.concatenate([w1, w2], axis=0)
        g = jnp.concatenate([jnp.concatenate([uu, ru.T], axis=1), jnp.concatenate([ru, rr], axis=1)], axis=0)
        tw = dot(g, w)
        w_s[t] = w
        t_s[t] = tw
        gram_s[t] = dot(w, tw, 0, 0)

    inverse_factors(gram_s, inv_s, fac_s)

    def store(t, which):
        src, dst = ((ubuf, nu_hbm), (vbuf, nv_hbm))[which]
        return pltpu.make_async_copy(src.at[t], dst.at[t], out_sem.at[which, t])

    for t in range(tiles):
        fac = fac_s[t]
        x = dot(w_s[t], fac, 1, 1) * scaling
        y = dot(t_s[t], fac, 1, 1) * (1.0 / scaling)
        c1 = y[:k]
        c2 = -dot(cores_ref[t], y[k:], 0, 0)
        x1, x2, c1, c2 = doubled(x[:k]), doubled(x[k:]), doubled(c1), doubled(c2)

        def finish(n, carry, t=t, x1=x1, x2=x2, c1=c1, c2=c2):
            at = pl.ds(pl.multiple_of(n * step, step), step)
            a = dotb(usp[t, at, :], x1) + dotb(rsp[at, :], x2)
            ubuf[t, at, :] = a[:, :k] + a[:, k:]
            b = dotb(vsp[t, at, :], c1) + dotb(csp[t, at, :], c2)
            vbuf[t, at, :] = b[:, :k] + b[:, k:]
            return carry

        lax.fori_loop(0, rows // step, finish, 0)
        store(t, 0).start()
        store(t, 1).start()
    for t in range(tiles):
        store(t, 0).wait()
        store(t, 1).wait()


def recompress(tile_u, tile_v, row_u, col_u, cores, sketch):
    tiles, rows, k = tile_u.shape
    vm = pl.BlockSpec(memory_space=pltpu.VMEM)
    hbm = pl.BlockSpec(memory_space=pl.ANY)
    out = jax.ShapeDtypeStruct(tile_u.shape, f32)
    return pl.pallas_call(
        local_kernel,
        name="recompress",
        out_shape=(out, out),
        in_specs=[hbm, hbm, vm, hbm, vm, vm],
        out_specs=(hbm, hbm),
        scratch_shapes=[
            pltpu.VMEM((tiles, rows, k), f32),
            pltpu.VMEM((tiles, rows, k), f32),
            pltpu.VMEM((tiles, rows, k), f32),
            pltpu.VMEM((tiles, rows, 2 * k), bf16),
            pltpu.VMEM((tiles, rows, 2 * k), bf16),
            pltpu.VMEM((tiles, rows, 2 * k), bf16),
            pltpu.VMEM((rows, 2 * k), bf16),
            pltpu.VMEM((2, 2 * k, rows), bf16),
            pltpu.VMEM((tiles, 2 * k, k), f32),
            pltpu.VMEM((tiles, 2 * k, k), f32),
            pltpu.VMEM((tiles, k, k), f32),
            pltpu.VMEM((tiles, k, k), f32),
            pltpu.VMEM((tiles, k, k), f32),
            pltpu.SemaphoreType.DMA((3, tiles)),
            pltpu.SemaphoreType.DMA((2, tiles)),
        ],
        compiler_params=pltpu.CompilerParams(vmem_limit_bytes=50 * 2**20),
        cost_estimate=pl.CostEstimate(flops=10**10, bytes_accessed=24 * 2**20, transcendentals=0),
    )(tile_u, tile_v, row_u, col_u, cores, sketch)


def side_by_side(arrays, axis, dim, along):
    widths = [a.shape[along] for a in arrays]
    both = jnp.concatenate(arrays, axis=along)
    filled = lax.all_gather(both, axis, axis=dim, tiled=True)
    return tuple(jnp.split(filled, [sum(widths[:k]) for k in range(1, len(widths))], axis=along))


def laid_out(parts, dim):
    parts = jnp.moveaxis(parts, 0, dim)
    shape = parts.shape
    return parts.reshape(*shape[:dim], shape[dim] * shape[dim + 1], *shape[dim + 2 :])


def from_everyone(x, axis):
    copies = jnp.broadcast_to(x, (lax.axis_size(axis), *x.shape))
    return lax.all_to_all(copies, axis, split_axis=0, concat_axis=0, tiled=True)


def gather_directly(x, axis, dim):
    return laid_out(from_everyone(x, axis), dim)


def split_up(x, dim, count):
    shape = x.shape
    parts = x.reshape(*shape[:dim], count, shape[dim] // count, *shape[dim + 1 :])
    return jnp.moveaxis(parts, dim, 0)


def sum_at_owner(x, axis, dim):
    parts = split_up(x, dim, lax.axis_size(axis))
    arrived = lax.all_to_all(parts, axis, split_axis=0, concat_axis=0, tiled=True)
    return arrived.sum(axis=0)


def body(tile_u, tile_v, row_panel_u, row_panel_v, col_panel_u, col_panel_v, diag_inverse, sketch):
    pieces = side_by_side((row_panel_v, col_panel_v), "col", 1, 0)
    first = jnp.einsum("ab,tbk->tak", diag_inverse, pieces[0], precision=highest)
    second = jnp.einsum("ab,tbk->tak", diag_inverse, pieces[1], precision=highest)
    col_u_rows, col_v_rows = side_by_side((col_panel_u, second), "row", 0, 1)
    row_u_full = gather_directly(row_panel_u, "col", 1)
    col_u_full = lax.all_to_all(col_u_rows, "col", split_axis=0, concat_axis=1, tiled=True)
    partial_cores = jnp.einsum("iak,jal->ijkl", first, col_v_rows, precision=highest)
    cores = sum_at_owner(partial_cores, "col", 1)
    new_u, new_v = recompress(tile_u[0], tile_v[0], row_u_full[0], col_u_full, cores[0], sketch)
    return new_u[None], new_v[None]


def solution(mesh):
    in_specs = (
        P("row", "col", None, None),
        P("row", "col", None, None),
        P("row", "col", None),
        P("row", "col", None),
        P("row", "col", None),
        P("row", "col", None),
        P("col", None),
        P(),
    )
    out_specs = (P("row", "col", None, None), P("row", "col", None, None))
    return jax.shard_map(body, mesh=mesh, in_specs=in_specs, out_specs=out_specs, check_vma=False)
```

```python
import math

import jax
import jax.numpy as jnp
from jax import lax
from jax.experimental import pallas as pl
from jax.experimental.pallas import tpu as pltpu
from jax.sharding import PartitionSpec as P

highest = lax.Precision.HIGHEST
f32, bf16 = jnp.float32, jnp.bfloat16


def halves(x):
    hi = x.astype(bf16)
    lo = (x - hi.astype(f32)).astype(bf16)
    return jnp.concatenate([hi, lo], axis=1)


def fold4(q):
    k = q.shape[0] // 2
    n = q.shape[1] // 2
    return q[:k, :n] + q[:k, n:] + q[k:, :n] + q[k:, n:]


def doubled(w):
    h = halves(w)
    return jnp.concatenate([h, h], axis=0)


def dot(a, b, ca=1, cb=0, precision=highest):
    return lax.dot_general(a, b, (((ca,), (cb,)), ((), ())), precision=precision, preferred_element_type=f32)


def dotb(a, b, ca=1, cb=0):
    return lax.dot_general(a, b, (((ca,), (cb,)), ((), ())), preferred_element_type=f32)


def inverse_factors(gram_ref, inv_ref, fac_ref):
    tiles, k, _ = gram_ref.shape
    row = lax.broadcasted_iota(jnp.int32, (tiles, 8, k), 1)
    lane = lax.broadcasted_iota(jnp.int32, (tiles, 8, k), 2)
    for p in range(k // 8):
        lo = 8 * p
        panel = gram_ref[:, lo : lo + 8, :]
        if p == 0:
            own = jnp.zeros((tiles, 8, k), f32)
        else:
            own = inv_ref[:, lo : lo + 8, :]
        own = own + jnp.where(lane == row + lo, 1.0, 0.0)
        cols = [jnp.broadcast_to(panel[:, :, lo + i : lo + i + 1], panel.shape) for i in range(8)]
        scale = jnp.zeros((tiles, 8, k), f32)
        pivot = jnp.zeros((tiles, 8, k), f32)
        for i in range(8):
            piv = jnp.broadcast_to(cols[i][:, i : i + 1, :], panel.shape)
            recip = 1.0 / piv
            scale = jnp.where(row == i, recip, scale)
            if i < 7:
                m = jnp.where(row > i, cols[i] * recip, 0.0)
                for j in range(i + 1, 8):
                    cols[j] = cols[j] - m * cols[j][:, i : i + 1, :]
                panel = panel - m * panel[:, i : i + 1, :]
                own = own - m * own[:, i : i + 1, :]
        fac_ref[:, lo : lo + 8, :] = own * jnp.sqrt(scale)
        if p < k // 8 - 1:
            lower = panel * scale
            for t in range(tiles):
                both = jnp.concatenate([panel[t], own[t]], axis=1)
                upd = dot(lower[t], both, 0, 0)
                gram_ref[t, lo + 8 :, :] = gram_ref[t, lo + 8 :, :] - upd[lo + 8 :, :k]
                if p == 0:
                    inv_ref[t, lo + 8 :, :] = -upd[lo + 8 :, k:]
                else:
                    inv_ref[t, lo + 8 :, :] = inv_ref[t, lo + 8 :, :] - upd[lo + 8 :, k:]


def local_kernel(u_hbm, v_hbm, r_ref, c_hbm, cores_ref, s_ref, nu_hbm, nv_hbm,
                 ubuf, vbuf, cbuf, usp, vsp, csp, rsp, tt, w_s, t_s, gram_s, inv_s, fac_s, in_sem, out_sem):
    tiles, rows, k = ubuf.shape
    step = min(512, rows)
    scaling = math.sqrt(rows)

    def load(t, which):
        src, dst = ((u_hbm, ubuf), (v_hbm, vbuf), (c_hbm, cbuf))[which]
        return pltpu.make_async_copy(src.at[t], dst.at[t], in_sem.at[which, t])

    for t in range(tiles):
        for which in range(3):
            load(t, which).start()

    for lo in range(0, rows, step):
        for n, ref in enumerate((r_ref, s_ref)):
            h = halves(ref[lo : lo + step, :])
            if n == 0:
                rsp[lo : lo + step, :] = h
            tt[n, :, lo : lo + step] = h.astype(f32).T.astype(bf16)
    rr = fold4(dotb(tt[0], rsp[...]))

    for t in range(tiles):
        for which in range(3):
            load(t, which).wait()
            buf, sp = ((ubuf, usp), (vbuf, vsp), (cbuf, csp))[which]

            def body(n, carry, buf=buf, sp=sp, t=t):
                at = pl.ds(pl.multiple_of(n * step, step), step)
                sp[t, at, :] = halves(buf[t, at, :])
                return carry

            lax.fori_loop(0, rows // step, body, 0)
        uu = fold4(dotb(usp[t], usp[t], 0, 0))
        ru = fold4(dotb(tt[0], usp[t]))
        p1t = fold4(dotb(tt[1], vsp[t]))
        p2t = fold4(dotb(tt[1], csp[t]))
        cores = cores_ref[t]
        w1 = p1t.T
        w2 = -dot(cores, p2t, 1, 1)
        w = jnp.concatenate([w1, w2], axis=0)
        g = jnp.concatenate([jnp.concatenate([uu, ru.T], axis=1), jnp.concatenate([ru, rr], axis=1)], axis=0)
        tw = dot(g, w)
        w_s[t] = w
        t_s[t] = tw
        gram_s[t] = dot(w, tw, 0, 0)

    inverse_factors(gram_s, inv_s, fac_s)

    def store(t, which):
        src, dst = ((ubuf, nu_hbm), (vbuf, nv_hbm))[which]
        return pltpu.make_async_copy(src.at[t], dst.at[t], out_sem.at[which, t])

    for t in range(tiles):
        fac = fac_s[t]
        x = dot(w_s[t], fac, 1, 1) * scaling
        y = dot(t_s[t], fac, 1, 1) * (1.0 / scaling)
        c1 = y[:k]
        c2 = -dot(cores_ref[t], y[k:], 0, 0)
        x1, x2, c1, c2 = doubled(x[:k]), doubled(x[k:]), doubled(c1), doubled(c2)

        def finish(n, carry, t=t, x1=x1, x2=x2, c1=c1, c2=c2):
            at = pl.ds(pl.multiple_of(n * step, step), step)
            a = dotb(usp[t, at, :], x1) + dotb(rsp[at, :], x2)
            ubuf[t, at, :] = a[:, :k] + a[:, k:]
            b = dotb(vsp[t, at, :], c1) + dotb(csp[t, at, :], c2)
            vbuf[t, at, :] = b[:, :k] + b[:, k:]
            return carry

        lax.fori_loop(0, rows // step, finish, 0)
        store(t, 0).start()
        store(t, 1).start()
    for t in range(tiles):
        store(t, 0).wait()
        store(t, 1).wait()


def recompress(tile_u, tile_v, row_u, col_u, cores, sketch):
    tiles, rows, k = tile_u.shape
    vm = pl.BlockSpec(memory_space=pltpu.VMEM)
    hbm = pl.BlockSpec(memory_space=pl.ANY)
    out = jax.ShapeDtypeStruct(tile_u.shape, f32)
    return pl.pallas_call(
        local_kernel,
        name="recompress",
        out_shape=(out, out),
        in_specs=[hbm, hbm, vm, hbm, vm, vm],
        out_specs=(hbm, hbm),
        scratch_shapes=[
            pltpu.VMEM((tiles, rows, k), f32),
            pltpu.VMEM((tiles, rows, k), f32),
            pltpu.VMEM((tiles, rows, k), f32),
            pltpu.VMEM((tiles, rows, 2 * k), bf16),
            pltpu.VMEM((tiles, rows, 2 * k), bf16),
            pltpu.VMEM((tiles, rows, 2 * k), bf16),
            pltpu.VMEM((rows, 2 * k), bf16),
            pltpu.VMEM((2, 2 * k, rows), bf16),
            pltpu.VMEM((tiles, 2 * k, k), f32),
            pltpu.VMEM((tiles, 2 * k, k), f32),
            pltpu.VMEM((tiles, k, k), f32),
            pltpu.VMEM((tiles, k, k), f32),
            pltpu.VMEM((tiles, k, k), f32),
            pltpu.SemaphoreType.DMA((3, tiles)),
            pltpu.SemaphoreType.DMA((2, tiles)),
        ],
        compiler_params=pltpu.CompilerParams(vmem_limit_bytes=50 * 2**20),
        cost_estimate=pl.CostEstimate(flops=10**10, bytes_accessed=24 * 2**20, transcendentals=0),
    )(tile_u, tile_v, row_u, col_u, cores, sketch)


MESH = pl.DeviceIdType.MESH
CENTRE, ACROSS, LEFT, RIGHT = 0, 1, 0, 1


class Links:
    def __init__(self, cols):
        self.r = lax.axis_index("row")
        self.c = lax.axis_index("col")
        self.cols = cols
        self.core = lax.rem(self.r, 2)
        self.m = lax.div(self.r, 2)
        self.x = lax.rem(self.m, 4)
        self.zl = lax.div(self.m, 4)

    def chip(self, zl, x):
        return 4 * zl + x

    def at_chip(self, m):
        return (2 * m + self.core, self.c)


def remote(src, dst, send, recv, device):
    return pltpu.make_async_remote_copy(
        src_ref=src, dst_ref=dst, send_sem=send, recv_sem=recv, device_id=device, device_id_type=MESH
    )


class Spread:
    def __init__(self, at, src, buf, sems, w):
        self.at, self.src, self.buf, self.w = at, src, buf, w
        (self.t_send, self.t_recv, self.z_send, self.z_recv, self.x_send, self.x_recv,
         self.f_send, self.f_recv, self.d_send, self.d_recv, self.own_sem) = sems
        self.rows = src.shape[1]
        self.other = (at.r + 1 - 2 * at.core, at.c)
        xl, xr = lax.rem(at.x + 3, 4), lax.rem(at.x + 1, 4)
        self.xs = (xl, xr)
        self.far = lax.rem(at.x + 2, 4)
        self.zls = (at.zl, 1 - at.zl)

    def block(self, m, core=None, tile=None):
        core = self.at.core if core is None else core
        rows = pl.ds(pl.multiple_of(m * self.rows, self.rows), self.rows)
        if tile is None:
            return self.buf.at[pl.ds(2 * core, 2), rows, :]
        return self.buf.at[pl.ds(2 * core + tile, 1), rows, :]

    def transpose_copy(self):
        at = self.at
        return remote(self.src, self.block(at.c), self.t_send.at[self.w], self.t_recv.at[self.w], (2 * at.c + at.core, at.m))

    def transpose_local(self):
        return pltpu.make_async_copy(self.src, self.block(self.at.c), self.own_sem.at[self.w])

    def transpose_start(self):
        @pl.when(self.at.m != self.at.c)
        def _():
            self.transpose_copy().start()

        @pl.when(self.at.m == self.at.c)
        def _():
            self.transpose_local().start()

    def transpose_wait(self):
        at = self.at

        @pl.when(at.m != at.c)
        def _():
            own = self.block(at.m)
            remote(own, own, self.t_send.at[self.w], self.t_recv.at[self.w], (2 * at.c + at.core, at.m)).wait_recv()

        @pl.when(at.m == at.c)
        def _():
            self.transpose_local().wait()

    def z_copy(self, zl):
        b = self.block(self.at.chip(zl, self.at.x))
        return remote(b, b, self.z_send.at[self.w], self.z_recv.at[self.w], self.at.at_chip(self.at.chip(self.zls[1], self.at.x)))

    def x_copy(self, s, to):
        b = self.block(self.at.chip(self.zls[s], self.at.x))
        return remote(b, b, self.x_send.at[self.w, s, to], self.x_recv.at[self.w, s, 1 - to], self.at.at_chip(self.at.chip(self.at.zl, self.xs[to])))

    def x_wait(self, s, came):
        b = self.block(self.at.chip(self.zls[s], self.xs[came]))
        remote(b, b, self.x_send.at[self.w, s, came], self.x_recv.at[self.w, s, came], self.other).wait_recv()

    def f_copy(self, s, came):
        b = self.block(self.at.chip(self.zls[s], self.xs[came]), tile=came)
        return remote(b, b, self.f_send.at[self.w, s, came], self.f_recv.at[self.w, s, came], self.at.at_chip(self.at.chip(self.at.zl, self.xs[1 - came])))

    def f_wait(self, s, came):
        b = self.block(self.at.chip(self.zls[s], self.far), tile=came)
        remote(b, b, self.f_send.at[self.w, s, came], self.f_recv.at[self.w, s, came], self.other).wait_recv()

    def d_copy(self, n, core=None):
        at = self.at
        core = at.core if core is None else core
        if n < 2:
            b = self.block(at.chip(self.zls[n], at.x), core)
        elif n < 6:
            s, came = divmod(n - 2, 2)
            b = self.block(at.chip(self.zls[s], self.xs[came]), core)
        else:
            s, came = divmod(n - 6, 2)
            b = self.block(at.chip(self.zls[s], self.far), core, came)
        return remote(b, b, self.d_send.at[self.w, n], self.d_recv.at[self.w, n], self.other)

    def stage_own(self):
        self.transpose_wait()
        self.x_copy(0, LEFT).start()
        self.x_copy(0, RIGHT).start()
        self.z_copy(self.zls[0]).start()
        self.d_copy(0).start()

    def stage_partner(self):
        self.z_copy(self.zls[1]).wait_recv()
        self.x_copy(1, LEFT).start()
        self.x_copy(1, RIGHT).start()
        self.d_copy(1).start()

    def stage_forward(self, s):
        for came in (LEFT, RIGHT):
            self.x_wait(s, came)
            self.f_copy(s, came).start()
            self.d_copy(2 + 2 * s + came).start()

    def stage_far(self, s):
        for came in (LEFT, RIGHT):
            self.f_wait(s, came)
            self.d_copy(6 + 2 * s + came).start()

    def stage_other_core(self):
        for n in range(10):
            self.d_copy(n, 1 - self.at.core).wait_recv()

    def drain(self):
        @pl.when(self.at.m != self.at.c)
        def _():
            self.transpose_copy().wait_send()

        self.z_copy(self.zls[0]).wait_send()
        for s in (0, 1):
            for to in (LEFT, RIGHT):
                self.x_copy(s, to).wait_send()
                self.f_copy(s, to).wait_send()
        for n in range(10):
            self.d_copy(n).wait_send()


def greet(at):
    barrier = pltpu.get_barrier_semaphore()

    def hello(device):
        pl.semaphore_signal(barrier, inc=1, device_id=device, device_id_type=MESH)

    for step in range(1, at.cols):
        hello((at.r, lax.rem(at.c + step, at.cols)))
    hello((at.r + 1 - 2 * at.core, at.c))
    hello(at.at_chip(at.chip(1 - at.zl, at.x)))
    hello(at.at_chip(at.chip(at.zl, lax.rem(at.x + 1, 4))))
    hello(at.at_chip(at.chip(at.zl, lax.rem(at.x + 3, 4))))

    @pl.when(at.m != at.c)
    def _():
        hello((2 * at.c + at.core, at.m))
        pl.semaphore_wait(barrier, at.cols + 4)

    @pl.when(at.m == at.c)
    def _():
        pl.semaphore_wait(barrier, at.cols + 3)


class Group:
    def __init__(self, at, send, recv):
        self.at, self.send, self.recv = at, send, recv

    def copy(self, src, dst, to):
        return remote(src, dst, self.send.at[to], self.recv.at[self.at.c], (self.at.r, to))

    def wait_from(self, dst, source):
        remote(dst, dst, self.send.at[source], self.recv.at[source], (self.at.r, source)).wait_recv()


def panel_kernel(rv_hbm, ru_hbm, cu_hbm, cv_hbm, d_hbm, cores_ref, r_hbm, c_hbm,
                 vblk, rbuf, dbuf, dsp, yacc, zpart, zsend, zt, zsp, cub, cvb, csp,
                 v_send, v_recv, r_send, r_recv, p_send, p_recv, q_send, q_recv,
                 t_send, t_recv, z_send, z_recv, x_send, x_recv, f_send, f_recv, d_send, d_recv, own_sem, in_sem, out_sem):
    cols, part, k = vblk.shape
    rows = cols * part
    at = Links(cols)
    sems = (t_send, t_recv, z_send, z_recv, x_send, x_recv, f_send, f_recv, d_send, d_recv, own_sem)
    cv = Spread(at, cv_hbm, cvb, sems, 0)
    cu = Spread(at, cu_hbm, cub, sems, 1)
    vg, rg, pg, qg = Group(at, v_send, v_recv), Group(at, r_send, r_recv), Group(at, p_send, p_recv), Group(at, q_send, q_recv)

    def rblock(b):
        return rbuf.at[pl.ds(pl.multiple_of(b * part, part), part), :]

    def others(do, keep=None):
        for step in range(1, cols):
            b = lax.rem(at.c + step, cols)
            if keep is None:
                do(b)
            else:
                pl.when(keep(b))(lambda b=b: do(b))

    later, earlier = (lambda b: b > at.c), (lambda b: b < at.c)
    load_d = pltpu.make_async_copy(d_hbm, dbuf, in_sem.at[0])
    load_v = pltpu.make_async_copy(rv_hbm.at[0], vblk.at[at.c], in_sem.at[1])
    load_r = pltpu.make_async_copy(ru_hbm.at[0], rblock(at.c), in_sem.at[2])
    load_d.start()
    load_v.start()
    load_r.start()
    greet(at)
    others(lambda b: vg.copy(rv_hbm.at[0], vblk.at[at.c], b).start(), later)
    cv.transpose_start()
    cu.transpose_start()
    others(lambda b: rg.copy(ru_hbm.at[0], rblock(at.c), b).start())

    load_d.wait()

    def split_d(b, carry):
        dsp[b] = halves(dbuf[:, pl.ds(pl.multiple_of(b * part, part), part)])
        return carry

    lax.fori_loop(0, at.c + 1, split_d, 0)
    cv.stage_own()

    def apply(b, first=False):
        vs = halves(vblk[b])
        q = dotb(dsp[b, :, :part], vs) + dotb(dsp[b, :, part:], vs)
        yacc[...] = q if first else yacc[...] + q

    load_v.wait()
    apply(at.c, True)

    def more(n, carry):
        b = at.c - 1 - n
        vg.wait_from(vblk.at[b], b)
        apply(b)
        return carry

    lax.fori_loop(0, at.c, more, 0)
    y = yacc[:, :k] + yacc[:, k:]
    yt = halves(y).astype(f32).T.astype(bf16)

    def back(b):
        q = dotb(yt, dsp[b])
        q = q[:k] + q[k:]
        return q[:, :part] + q[:, part:]

    def send_back(n, carry):
        zsend[n] = back(n)
        pg.copy(zsend.at[n], zpart.at[at.c], n).start()
        return carry

    lax.fori_loop(0, at.c, send_back, 0)
    cv.stage_partner()
    zt[at.c] = back(at.c)
    cv.stage_forward(0)

    def gather(n, carry):
        b = cols - 1 - n
        pg.wait_from(zpart.at[b], b)
        zt[at.c] = zt[at.c] + zpart[b]
        return carry

    lax.fori_loop(0, cols - 1 - at.c, gather, 0)
    others(lambda b: qg.copy(zt.at[at.c], zt.at[at.c], b).start())
    cv.stage_forward(1)
    cu.stage_own()
    cv.stage_far(0)
    cv.stage_far(1)
    cu.stage_partner()
    others(lambda b: qg.wait_from(zt.at[b], b))
    for b in range(cols):
        z = zt[b]
        hi = z.astype(bf16)
        zsp[:k, part * b : part * (b + 1)] = hi
        zsp[k:, part * b : part * (b + 1)] = (z - hi.astype(f32)).astype(bf16)
    cu.stage_forward(0)
    cv.stage_other_core()
    for t in range(cores_ref.shape[0]):

        def split_c(n, carry, t=t):
            ds = pl.ds(pl.multiple_of(n * part, part), part)
            csp[ds, :] = halves(cvb[t, ds, :])
            return carry

        lax.fori_loop(0, cols, split_c, 0)
        cores_ref[t] = fold4(dotb(zsp[...], csp[...]))
        if t == 0:
            cu.stage_forward(1)
    cu.stage_far(0)
    cu.stage_far(1)
    load_r.wait()
    others(lambda b: rg.wait_from(rblock(b), b))
    out_r = pltpu.make_async_copy(rbuf, r_hbm, out_sem.at[0])
    out_r.start()
    cu.stage_other_core()
    out_c = pltpu.make_async_copy(cub, c_hbm, out_sem.at[1])
    out_c.start()

    others(lambda b: vg.copy(rv_hbm.at[0], vblk.at[at.c], b).wait_send(), later)
    others(lambda b: rg.copy(ru_hbm.at[0], rblock(at.c), b).wait_send())
    others(lambda b: pg.copy(zsend.at[b], zpart.at[at.c], b).wait_send(), earlier)
    others(lambda b: qg.copy(zt.at[at.c], zt.at[at.c], b).wait_send())
    cv.drain()
    cu.drain()
    out_r.wait()
    out_c.wait()


def spread_panels(row_v, row_u, col_u, col_v, diag, tiles):
    cols = lax.axis_size("col")
    part, k = row_v.shape[1:]
    rows = cols * part
    vm = pl.BlockSpec(memory_space=pltpu.VMEM)
    hbm = pl.BlockSpec(memory_space=pl.ANY)
    dma = pltpu.SemaphoreType.DMA
    return pl.pallas_call(
        panel_kernel,
        name="spread_panels",
        out_shape=(
            jax.ShapeDtypeStruct((tiles, k, k), f32),
            jax.ShapeDtypeStruct((rows, k), f32),
            jax.ShapeDtypeStruct((tiles, rows, k), f32),
        ),
        in_specs=[hbm] * 5,
        out_specs=(vm, hbm, hbm),
        scratch_shapes=[
            pltpu.VMEM((cols, part, k), f32),
            pltpu.VMEM((rows, k), f32),
            pltpu.VMEM((part, rows), f32),
            pltpu.VMEM((cols, part, 2 * part), bf16),
            pltpu.VMEM((part, 2 * k), f32),
            pltpu.VMEM((cols, k, part), f32),
            pltpu.VMEM((cols, k, part), f32),
            pltpu.VMEM((cols, k, part), f32),
            pltpu.VMEM((2 * k, rows), bf16),
            pltpu.VMEM((tiles, rows, k), f32),
            pltpu.VMEM((tiles, rows, k), f32),
            pltpu.VMEM((rows, 2 * k), bf16),
        ]
        + [dma((cols,))] * 8
        + [dma((2,))] * 4
        + [dma((2, 2, 2))] * 4
        + [dma((2, 10))] * 2
        + [dma((2,)), dma((3,)), dma((2,))],
        compiler_params=pltpu.CompilerParams(collective_id=0, has_side_effects=True, vmem_limit_bytes=50 * 2**20),
        cost_estimate=pl.CostEstimate(flops=10**9, bytes_accessed=16 * 2**20, transcendentals=0),
    )(row_v, row_u, col_u, col_v, diag)


def body(tile_u, tile_v, row_panel_u, row_panel_v, col_panel_u, col_panel_v, diag_inverse, sketch):
    cores, row_u, col_u = spread_panels(row_panel_v, row_panel_u, col_panel_u, col_panel_v, diag_inverse, tile_u.shape[1])
    new_u, new_v = recompress(tile_u[0], tile_v[0], row_u, col_u, cores, sketch)
    return new_u[None], new_v[None]


def solution(mesh):
    in_specs = (
        P("row", "col", None, None),
        P("row", "col", None, None),
        P("row", "col", None),
        P("row", "col", None),
        P("row", "col", None),
        P("row", "col", None),
        P("col", None),
        P(),
    )
    out_specs = (P("row", "col", None, None), P("row", "col", None, None))
    return jax.shard_map(body, mesh=mesh, in_specs=in_specs, out_specs=out_specs, check_vma=False)
```

```python
import math

import jax
import jax.numpy as jnp
from jax import lax
from jax.experimental import pallas as pl
from jax.experimental.pallas import tpu as pltpu
from jax.sharding import PartitionSpec as P

highest = lax.Precision.HIGHEST
f32, bf16 = jnp.float32, jnp.bfloat16


def halves(x):
    hi = x.astype(bf16)
    lo = (x - hi.astype(f32)).astype(bf16)
    return jnp.concatenate([hi, lo], axis=1)


def fold4(q):
    k = q.shape[0] // 2
    n = q.shape[1] // 2
    return q[:k, :n] + q[:k, n:] + q[k:, :n] + q[k:, n:]


def doubled(w):
    h = halves(w)
    return jnp.concatenate([h, h], axis=0)


def dot(a, b, ca=1, cb=0, precision=highest):
    return lax.dot_general(a, b, (((ca,), (cb,)), ((), ())), precision=precision, preferred_element_type=f32)


def dotb(a, b, ca=1, cb=0):
    return lax.dot_general(a, b, (((ca,), (cb,)), ((), ())), preferred_element_type=f32)


def inverse_factors(gram_ref, inv_ref, fac_ref):
    tiles, k, _ = gram_ref.shape
    row = lax.broadcasted_iota(jnp.int32, (tiles, 8, k), 1)
    lane = lax.broadcasted_iota(jnp.int32, (tiles, 8, k), 2)
    for p in range(k // 8):
        lo = 8 * p
        panel = gram_ref[:, lo : lo + 8, :]
        if p == 0:
            own = jnp.zeros((tiles, 8, k), f32)
        else:
            own = inv_ref[:, lo : lo + 8, :]
        own = own + jnp.where(lane == row + lo, 1.0, 0.0)
        cols = [jnp.broadcast_to(panel[:, :, lo + i : lo + i + 1], panel.shape) for i in range(8)]
        scale = jnp.zeros((tiles, 8, k), f32)
        pivot = jnp.zeros((tiles, 8, k), f32)
        for i in range(8):
            piv = jnp.broadcast_to(cols[i][:, i : i + 1, :], panel.shape)
            recip = 1.0 / piv
            scale = jnp.where(row == i, recip, scale)
            if i < 7:
                m = jnp.where(row > i, cols[i] * recip, 0.0)
                for j in range(i + 1, 8):
                    cols[j] = cols[j] - m * cols[j][:, i : i + 1, :]
                panel = panel - m * panel[:, i : i + 1, :]
                own = own - m * own[:, i : i + 1, :]
        fac_ref[:, lo : lo + 8, :] = own * jnp.sqrt(scale)
        if p < k // 8 - 1:
            lower = panel * scale
            for t in range(tiles):
                both = jnp.concatenate([panel[t], own[t]], axis=1)
                upd = dot(lower[t], both, 0, 0)
                gram_ref[t, lo + 8 :, :] = gram_ref[t, lo + 8 :, :] - upd[lo + 8 :, :k]
                if p == 0:
                    inv_ref[t, lo + 8 :, :] = -upd[lo + 8 :, k:]
                else:
                    inv_ref[t, lo + 8 :, :] = inv_ref[t, lo + 8 :, :] - upd[lo + 8 :, k:]


def finish_kernel(u_hbm, v_hbm, r_hbm, c_hbm, cores_hbm, w_hbm, t_hbm, gram_hbm, nu_hbm, nv_hbm,
                  ubuf, vbuf, cbuf, rbuf, cores_ref, w_ref, t_ref, gram_s, inv_s, fac_s, in_sem, r_sem, out_sem):
    tiles, rows, k = ubuf.shape
    step = min(512, rows)
    scaling = math.sqrt(rows)

    def load(t, which):
        src, dst = ((u_hbm, ubuf), (v_hbm, vbuf), (c_hbm, cbuf))[which]
        return pltpu.make_async_copy(src.at[t], dst.at[t], in_sem.at[which, t])

    singles = [
        pltpu.make_async_copy(src, dst, r_sem.at[n])
        for n, (src, dst) in enumerate(((gram_hbm, gram_s), (w_hbm, w_ref), (t_hbm, t_ref), (cores_hbm, cores_ref), (r_hbm, rbuf)))
    ]
    for copy in singles:
        copy.start()
    for t in range(tiles):
        for which in range(3):
            load(t, which).start()
    singles[0].wait()
    inverse_factors(gram_s, inv_s, fac_s)

    def store(t, which):
        src, dst = ((ubuf, nu_hbm), (vbuf, nv_hbm))[which]
        return pltpu.make_async_copy(src.at[t], dst.at[t], out_sem.at[which, t])

    for copy in singles[1:]:
        copy.wait()
    for t in range(tiles):
        for which in range(3):
            load(t, which).wait()
        fac = fac_s[t]
        x = dot(w_ref[t], fac, 1, 1) * scaling
        y = dot(t_ref[t], fac, 1, 1) * (1.0 / scaling)
        c1 = y[:k]
        c2 = -dot(cores_ref[t], y[k:], 0, 0)
        x1, x2, c1, c2 = doubled(x[:k]), doubled(x[k:]), doubled(c1), doubled(c2)

        def finish(n, carry, t=t, x1=x1, x2=x2, c1=c1, c2=c2):
            at = pl.ds(pl.multiple_of(n * step, step), step)
            a = dotb(halves(ubuf[t, at, :]), x1) + dotb(halves(rbuf[at, :]), x2)
            ubuf[t, at, :] = a[:, :k] + a[:, k:]
            b = dotb(halves(vbuf[t, at, :]), c1) + dotb(halves(cbuf[t, at, :]), c2)
            vbuf[t, at, :] = b[:, :k] + b[:, k:]
            return carry

        lax.fori_loop(0, rows // step, finish, 0)
        store(t, 0).start()
        store(t, 1).start()
    for t in range(tiles):
        store(t, 0).wait()
        store(t, 1).wait()


def recompress(tile_u, tile_v, row_u, col_u, cores, w, tw, gram):
    tiles, rows, k = tile_u.shape
    hbm = pl.BlockSpec(memory_space=pltpu.HBM)
    out = jax.ShapeDtypeStruct(tile_u.shape, f32)
    return pl.pallas_call(
        finish_kernel,
        name="recompress",
        out_shape=(out, out),
        in_specs=[hbm] * 8,
        out_specs=(hbm, hbm),
        scratch_shapes=[
            pltpu.VMEM((tiles, rows, k), f32),
            pltpu.VMEM((tiles, rows, k), f32),
            pltpu.VMEM((tiles, rows, k), f32),
            pltpu.VMEM((rows, k), f32),
            pltpu.VMEM((tiles, k, k), f32),
            pltpu.VMEM((tiles, 2 * k, k), f32),
            pltpu.VMEM((tiles, 2 * k, k), f32),
            pltpu.VMEM((tiles, k, k), f32),
            pltpu.VMEM((tiles, k, k), f32),
            pltpu.VMEM((tiles, k, k), f32),
            pltpu.SemaphoreType.DMA((3, tiles)),
            pltpu.SemaphoreType.DMA((5,)),
            pltpu.SemaphoreType.DMA((2, tiles)),
        ],
        compiler_params=pltpu.CompilerParams(vmem_limit_bytes=60 * 2**20),
        cost_estimate=pl.CostEstimate(flops=10**10, bytes_accessed=24 * 2**20, transcendentals=0),
    )(tile_u, tile_v, row_u, col_u, cores, w, tw, gram)


MESH = pl.DeviceIdType.MESH
CENTRE, ACROSS, LEFT, RIGHT = 0, 1, 0, 1


def mix(a, b):
    out = 0
    for bit in (4, 2, 1):
        out = out + bit * lax.rem(lax.div(a, bit) + lax.div(b, bit), 2)
    return out


class Links:
    def __init__(self, cols):
        self.r = lax.axis_index("row")
        self.c = lax.axis_index("col")
        self.cols = cols
        self.core = lax.rem(self.r, 2)
        self.m = lax.div(self.r, 2)
        self.x = lax.rem(self.m, 4)
        self.zl = lax.div(self.m, 4)
        self.mixed = mix(self.m, self.c)
        self.target = (2 * self.mixed + self.core, self.m)
        self.source = (2 * self.c + self.core, self.mixed)
        self.alone = jnp.logical_and(self.m == 0, self.c == 0)

    def chip(self, zl, x):
        return 4 * zl + x

    def at_chip(self, m):
        return (2 * m + self.core, self.c)


def remote(src, dst, send, recv, device):
    return pltpu.make_async_remote_copy(
        src_ref=src, dst_ref=dst, send_sem=send, recv_sem=recv, device_id=device, device_id_type=MESH
    )


class Spread:
    def __init__(self, at, src, buf, sems, w):
        self.at, self.src, self.buf, self.w = at, src, buf, w
        (self.t_send, self.t_recv, self.z_send, self.z_recv, self.x_send, self.x_recv,
         self.f_send, self.f_recv, self.d_send, self.d_recv, self.own_sem) = sems
        self.rows = src.shape[1]
        self.other = (at.r + 1 - 2 * at.core, at.c)
        xl, xr = lax.rem(at.x + 3, 4), lax.rem(at.x + 1, 4)
        self.xs = (xl, xr)
        self.far = lax.rem(at.x + 2, 4)
        self.zls = (at.zl, 1 - at.zl)

    def block(self, m, core=None, tile=None):
        core = self.at.core if core is None else core
        rows = pl.ds(pl.multiple_of(mix(m, self.at.c) * self.rows, self.rows), self.rows)
        if tile is None:
            return self.buf.at[pl.ds(2 * core, 2), rows, :]
        return self.buf.at[pl.ds(2 * core + tile, 1), rows, :]

    def transpose_copy(self):
        at = self.at
        rows = pl.ds(pl.multiple_of(at.c * self.rows, self.rows), self.rows)
        dst = self.buf.at[pl.ds(2 * at.core, 2), rows, :]
        return remote(self.src, dst, self.t_send.at[self.w], self.t_recv.at[self.w], at.target)

    def transpose_local(self):
        return pltpu.make_async_copy(self.src, self.block(self.at.m), self.own_sem.at[self.w])

    def transpose_start(self):
        @pl.when(jnp.logical_not(self.at.alone))
        def _():
            self.transpose_copy().start()

        @pl.when(self.at.alone)
        def _():
            self.transpose_local().start()

    def transpose_wait(self):
        at = self.at

        @pl.when(jnp.logical_not(at.alone))
        def _():
            own = self.block(at.m)
            remote(own, own, self.t_send.at[self.w], self.t_recv.at[self.w], at.source).wait_recv()

        @pl.when(at.alone)
        def _():
            self.transpose_local().wait()

    def z_copy(self, zl):
        b = self.block(self.at.chip(zl, self.at.x))
        return remote(b, b, self.z_send.at[self.w], self.z_recv.at[self.w], self.at.at_chip(self.at.chip(self.zls[1], self.at.x)))

    def x_copy(self, s, to):
        b = self.block(self.at.chip(self.zls[s], self.at.x))
        return remote(b, b, self.x_send.at[self.w, s, to], self.x_recv.at[self.w, s, 1 - to], self.at.at_chip(self.at.chip(self.at.zl, self.xs[to])))

    def x_wait(self, s, came):
        b = self.block(self.at.chip(self.zls[s], self.xs[came]))
        remote(b, b, self.x_send.at[self.w, s, came], self.x_recv.at[self.w, s, came], self.other).wait_recv()

    def f_copy(self, s, came):
        b = self.block(self.at.chip(self.zls[s], self.xs[came]), tile=came)
        return remote(b, b, self.f_send.at[self.w, s, came], self.f_recv.at[self.w, s, came], self.at.at_chip(self.at.chip(self.at.zl, self.xs[1 - came])))

    def f_wait(self, s, came):
        b = self.block(self.at.chip(self.zls[s], self.far), tile=came)
        remote(b, b, self.f_send.at[self.w, s, came], self.f_recv.at[self.w, s, came], self.other).wait_recv()

    def d_copy(self, n, core=None):
        at = self.at
        core = at.core if core is None else core
        if n < 2:
            b = self.block(at.chip(self.zls[n], at.x), core)
        elif n < 6:
            s, came = divmod(n - 2, 2)
            b = self.block(at.chip(self.zls[s], self.xs[came]), core)
        else:
            s, came = divmod(n - 6, 2)
            b = self.block(at.chip(self.zls[s], self.far), core, came)
        return remote(b, b, self.d_send.at[self.w, n], self.d_recv.at[self.w, n], self.other)

    def stage_own(self):
        self.transpose_wait()
        self.x_copy(0, LEFT).start()
        self.x_copy(0, RIGHT).start()
        self.z_copy(self.zls[0]).start()
        self.d_copy(0).start()

    def stage_partner(self):
        self.z_copy(self.zls[1]).wait_recv()
        self.x_copy(1, LEFT).start()
        self.x_copy(1, RIGHT).start()
        self.d_copy(1).start()

    def stage_forward(self, s):
        for came in (LEFT, RIGHT):
            self.x_wait(s, came)
            self.f_copy(s, came).start()
            self.d_copy(2 + 2 * s + came).start()

    def stage_far(self, s):
        for came in (LEFT, RIGHT):
            self.f_wait(s, came)
            self.d_copy(6 + 2 * s + came).start()

    def stage_other_core(self):
        for n in range(10):
            self.d_copy(n, 1 - self.at.core).wait_recv()

    def drain(self):
        @pl.when(jnp.logical_not(self.at.alone))
        def _():
            self.transpose_copy().wait_send()

        self.z_copy(self.zls[0]).wait_send()
        for s in (0, 1):
            for to in (LEFT, RIGHT):
                self.x_copy(s, to).wait_send()
                self.f_copy(s, to).wait_send()
        for n in range(10):
            self.d_copy(n).wait_send()


def greet(at):
    barrier = pltpu.get_barrier_semaphore()

    def hello(device):
        pl.semaphore_signal(barrier, inc=1, device_id=device, device_id_type=MESH)

    for step in range(1, at.cols):
        hello((at.r, lax.rem(at.c + step, at.cols)))
    hello((at.r + 1 - 2 * at.core, at.c))
    hello(at.at_chip(at.chip(1 - at.zl, at.x)))
    hello(at.at_chip(at.chip(at.zl, lax.rem(at.x + 1, 4))))
    hello(at.at_chip(at.chip(at.zl, lax.rem(at.x + 3, 4))))

    @pl.when(jnp.logical_not(at.alone))
    def _():
        hello(at.target)
        hello(at.source)
        pl.semaphore_wait(barrier, at.cols + 5)

    @pl.when(at.alone)
    def _():
        pl.semaphore_wait(barrier, at.cols + 3)


class Group:
    def __init__(self, at, send, recv):
        self.at, self.send, self.recv = at, send, recv

    def copy(self, src, dst, to):
        return remote(src, dst, self.send.at[to], self.recv.at[self.at.c], (self.at.r, to))

    def wait_from(self, dst, source):
        remote(dst, dst, self.send.at[source], self.recv.at[source], (self.at.r, source)).wait_recv()


class Tree:
    def __init__(self, at, block, sems):
        self.at, self.block = at, block
        self.z_send, self.z_recv, self.y_send, self.y_recv, self.f_send, self.f_recv = sems
        y, zh = lax.div(at.c, 2), lax.rem(at.c, 2)
        self.zhs = (zh, 1 - zh)
        self.ys = (lax.rem(y + 3, 4), lax.rem(y + 1, 4))
        self.y, self.far = y, lax.rem(y + 2, 4)

    def col(self, y, s):
        return 2 * y + self.zhs[s]

    def z_copy(self, s):
        b = self.block(self.col(self.y, s))
        return remote(b, b, self.z_send.at[0], self.z_recv.at[0], (self.at.r, self.col(self.y, 1)))

    def y_copy(self, s, to):
        b = self.block(self.col(self.y, s))
        return remote(b, b, self.y_send.at[s, to], self.y_recv.at[s, 1 - to], (self.at.r, self.col(self.ys[to], 0)))

    def y_wait(self, s, came):
        b = self.block(self.col(self.ys[came], s))
        remote(b, b, self.y_send.at[s, came], self.y_recv.at[s, came], (self.at.r, self.col(self.ys[came], 0))).wait_recv()

    def f_copy(self, s, came):
        b = self.block(self.col(self.ys[came], s), came)
        return remote(b, b, self.f_send.at[s, came], self.f_recv.at[s, came], (self.at.r, self.col(self.ys[1 - came], 0)))

    def f_wait(self, s, came):
        b = self.block(self.col(self.far, s), came)
        remote(b, b, self.f_send.at[s, came], self.f_recv.at[s, came], (self.at.r, self.col(self.ys[came], 0))).wait_recv()

    def stage_own(self):
        self.z_copy(0).start()
        self.y_copy(0, LEFT).start()
        self.y_copy(0, RIGHT).start()

    def stage_partner(self):
        self.z_copy(1).wait_recv()
        self.y_copy(1, LEFT).start()
        self.y_copy(1, RIGHT).start()

    def stage_forward(self, s):
        for came in (LEFT, RIGHT):
            self.y_wait(s, came)
            self.f_copy(s, came).start()

    def stage_far(self, s):
        for came in (LEFT, RIGHT):
            self.f_wait(s, came)

    def drain(self):
        self.z_copy(0).wait_send()
        for s in (0, 1):
            for to in (LEFT, RIGHT):
                self.y_copy(s, to).wait_send()
                self.f_copy(s, to).wait_send()


def panel_kernel(rv_hbm, ru_hbm, cu_hbm, cv_hbm, d_hbm, u_hbm, v_hbm, s_ref, w_ref, t_ref, gram_ref, cores_ref, r_hbm, c_hbm,
                 vblk, vsp, rbuf, rsp, dbuf, dsp, zpart, zsend, zt, zsp, cub, cvb, csp, ubuf, vbuf, usp, tts, ttr, uu_s, p1_s, ru_s,
                 v_send, v_recv, p_send, p_recv, rz_send, rz_recv, ry_send, ry_recv, rf_send, rf_recv,
                 qz_send, qz_recv, qy_send, qy_recv, qf_send, qf_recv,
                 t_send, t_recv, z_send, z_recv, x_send, x_recv, f_send, f_recv, d_send, d_recv, own_sem, in_sem, out_sem, uv_sem):
    cols, part, k = vblk.shape
    tiles = ubuf.shape[0]
    rows = cols * part
    at = Links(cols)
    sems = (t_send, t_recv, z_send, z_recv, x_send, x_recv, f_send, f_recv, d_send, d_recv, own_sem)
    cv = Spread(at, cv_hbm, cvb, sems, 0)
    cu = Spread(at, cu_hbm, cub, sems, 1)
    vg, pg = Group(at, v_send, v_recv), Group(at, p_send, p_recv)

    def span(b):
        return pl.ds(pl.multiple_of(b * part, part), part)

    def rblock(b, half=None):
        if half is None:
            return rbuf.at[span(b), :]
        size = part // 2
        return rbuf.at[pl.ds(pl.multiple_of(b * part + half * size, size), size), :]

    def zblock(b, half=None):
        if half is None:
            return zt.at[b]
        size = k // 2
        return zt.at[b, size * half : size * (half + 1), :]

    rg = Tree(at, rblock, (rz_send, rz_recv, ry_send, ry_recv, rf_send, rf_recv))
    qg = Tree(at, zblock, (qz_send, qz_recv, qy_send, qy_recv, qf_send, qf_recv))

    def others(do, keep=None):
        for step in range(1, cols):
            b = lax.rem(at.c + step, cols)
            if keep is None:
                do(b)
            else:

                @pl.when(keep(b))
                def _(b=b):
                    do(b)

    later, earlier = (lambda b: b > at.c), (lambda b: b < at.c)
    load_d = pltpu.make_async_copy(d_hbm, dbuf, in_sem.at[0])
    load_v = pltpu.make_async_copy(rv_hbm.at[0], vblk.at[at.c], in_sem.at[1])
    load_r = pltpu.make_async_copy(ru_hbm.at[0], rblock(at.c), in_sem.at[2])

    def load_tile(t, which):
        src, dst = ((u_hbm, ubuf), (v_hbm, vbuf))[which]
        return pltpu.make_async_copy(src.at[t], dst.at[t], uv_sem.at[which, t])

    load_d.start()
    load_v.start()
    load_r.start()
    greet(at)
    others(lambda b: vg.copy(rv_hbm.at[0], vblk.at[at.c], b).start(), later)
    cv.transpose_start()
    cu.transpose_start()
    for t in range(tiles):
        load_tile(t, 0).start()
        load_tile(t, 1).start()

    for b in range(cols):

        @pl.when(b > at.c)
        def _(b=b):
            vsp[part * b : part * (b + 1), :] = jnp.zeros((part, 2 * k), bf16)

    load_d.wait()

    def split_d(b, carry):
        d = dbuf[:, span(b)]
        hi = d.astype(bf16)
        dsp[0, :, span(b)] = hi
        dsp[1, :, span(b)] = (d - hi.astype(f32)).astype(bf16)
        return carry

    lax.fori_loop(0, cols, split_d, 0)

    def split_s(b, carry):
        tts[:, span(b)] = halves(s_ref[span(b), :]).astype(f32).T.astype(bf16)
        return carry

    lax.fori_loop(0, cols, split_s, 0)

    def split_into(dst, src):
        def body(b, carry):
            dst[span(b), :] = halves(src[span(b), :])
            return carry

        lax.fori_loop(0, cols, body, 0)

    def tile_products(t):
        load_tile(t, 0).wait()
        load_tile(t, 1).wait()
        split_into(usp.at[t], ubuf.at[t])
        uu_s[t] = fold4(dotb(usp[t], usp[t], 0, 0))
        split_into(csp, vbuf.at[t])
        p1_s[t] = fold4(dotb(tts[...], csp[...]))

    cv.stage_own()
    cu.stage_own()
    load_v.wait()
    vsp[span(at.c), :] = halves(vblk[at.c])

    def arrived(b, carry):
        vg.wait_from(vblk.at[b], b)
        vsp[span(b), :] = halves(vblk[b])
        return carry

    lax.fori_loop(0, at.c, arrived, 0)
    q = dotb(dsp[0], vsp[...]) + dotb(dsp[1], vsp[...])
    yt = halves(q[:, :k] + q[:, k:]).astype(f32).T.astype(bf16)
    for b in range(cols):
        q = dotb(yt, dsp[0, :, part * b : part * (b + 1)]) + dotb(yt, dsp[1, :, part * b : part * (b + 1)])
        zsend[b] = q[:k] + q[k:]
    others(lambda b: pg.copy(zsend.at[b], zpart.at[at.c], b).start(), earlier)
    cv.stage_partner()
    cu.stage_partner()
    load_r.wait()
    rg.stage_own()
    tile_products(0)
    cv.stage_forward(0)
    cu.stage_forward(0)
    zt[at.c] = zsend[at.c]

    def gather(n, carry):
        b = cols - 1 - n
        pg.wait_from(zpart.at[b], b)
        zt[at.c] = zt[at.c] + zpart[b]
        return carry

    lax.fori_loop(0, cols - 1 - at.c, gather, 0)
    qg.stage_own()
    rg.stage_partner()
    tile_products(1)
    qg.stage_partner()
    cv.stage_forward(1)
    cu.stage_forward(1)
    rg.stage_forward(0)
    qg.stage_forward(0)
    tile_products(2)
    rg.stage_forward(1)
    qg.stage_forward(1)
    tile_products(3)
    cv.stage_far(0)
    cu.stage_far(0)
    cv.stage_far(1)
    cu.stage_far(1)
    rg.stage_far(0)
    rg.stage_far(1)
    out_r = pltpu.make_async_copy(rbuf, r_hbm, out_sem.at[0])
    out_r.start()

    def split_r(b, carry):
        h = halves(rbuf[span(b), :])
        rsp[span(b), :] = h
        ttr[:, span(b)] = h.astype(f32).T.astype(bf16)
        return carry

    lax.fori_loop(0, cols, split_r, 0)
    rr = fold4(dotb(ttr[...], rsp[...]))
    for t in range(tiles):
        ru_s[t] = fold4(dotb(ttr[...], usp[t]))
    qg.stage_far(0)
    qg.stage_far(1)
    for b in range(cols):
        z = zt[b]
        hi = z.astype(bf16)
        zsp[:k, part * b : part * (b + 1)] = hi
        zsp[k:, part * b : part * (b + 1)] = (z - hi.astype(f32)).astype(bf16)
    cv.stage_other_core()
    for t in range(tiles):
        split_into(csp, cvb.at[t])
        cores_ref[t] = fold4(dotb(zsp[...], csp[...]))
    cu.stage_other_core()
    out_c = pltpu.make_async_copy(cub, c_hbm, out_sem.at[1])
    out_c.start()
    for t in range(tiles):
        split_into(csp, cub.at[t])
        p2t = fold4(dotb(tts[...], csp[...]))
        w1 = p1_s[t].T
        w2 = -dot(cores_ref[t], p2t, 1, 1)
        w = jnp.concatenate([w1, w2], axis=0)
        ru = ru_s[t]
        g = jnp.concatenate([jnp.concatenate([uu_s[t], ru.T], axis=1), jnp.concatenate([ru, rr], axis=1)], axis=0)
        tw = dot(g, w)
        w_ref[t] = w
        t_ref[t] = tw
        gram_ref[t] = dot(w, tw, 0, 0)

    others(lambda b: vg.copy(rv_hbm.at[0], vblk.at[at.c], b).wait_send(), later)
    others(lambda b: pg.copy(zsend.at[b], zpart.at[at.c], b).wait_send(), earlier)
    rg.drain()
    qg.drain()
    cv.drain()
    cu.drain()
    out_r.wait()
    out_c.wait()


def spread_panels(row_v, row_u, col_u, col_v, diag, tile_u, tile_v, sketch):
    cols = lax.axis_size("col")
    tiles = tile_u.shape[0]
    part, k = row_v.shape[1:]
    rows = cols * part
    vm = pl.BlockSpec(memory_space=pltpu.VMEM)
    hbm = pl.BlockSpec(memory_space=pltpu.HBM)
    dma = pltpu.SemaphoreType.DMA
    return pl.pallas_call(
        panel_kernel,
        name="spread_panels",
        out_shape=(
            jax.ShapeDtypeStruct((tiles, 2 * k, k), f32),
            jax.ShapeDtypeStruct((tiles, 2 * k, k), f32),
            jax.ShapeDtypeStruct((tiles, k, k), f32),
            jax.ShapeDtypeStruct((tiles, k, k), f32),
            jax.ShapeDtypeStruct((rows, k), f32),
            jax.ShapeDtypeStruct((tiles, rows, k), f32),
        ),
        in_specs=[hbm] * 7 + [vm],
        out_specs=(vm, vm, vm, vm, hbm, hbm),
        scratch_shapes=[
            pltpu.VMEM((cols, part, k), f32),
            pltpu.VMEM((rows, 2 * k), bf16),
            pltpu.VMEM((rows, k), f32),
            pltpu.VMEM((rows, 2 * k), bf16),
            pltpu.VMEM((part, rows), f32),
            pltpu.VMEM((2, part, rows), bf16),
            pltpu.VMEM((cols, k, part), f32),
            pltpu.VMEM((cols, k, part), f32),
            pltpu.VMEM((cols, k, part), f32),
            pltpu.VMEM((2 * k, rows), bf16),
            pltpu.VMEM((tiles, rows, k), f32),
            pltpu.VMEM((tiles, rows, k), f32),
            pltpu.VMEM((rows, 2 * k), bf16),
            pltpu.VMEM((tiles, rows, k), f32),
            pltpu.VMEM((tiles, rows, k), f32),
            pltpu.VMEM((tiles, rows, 2 * k), bf16),
            pltpu.VMEM((2 * k, rows), bf16),
            pltpu.VMEM((2 * k, rows), bf16),
            pltpu.VMEM((tiles, k, k), f32),
            pltpu.VMEM((tiles, k, k), f32),
            pltpu.VMEM((tiles, k, k), f32),
        ]
        + [dma((cols,))] * 4
        + ([dma((1,))] * 2 + [dma((2, 2))] * 4) * 2
        + [dma((2,))] * 4
        + [dma((2, 2, 2))] * 4
        + [dma((2, 10))] * 2
        + [dma((2,)), dma((3,)), dma((2,)), dma((2, tiles))],
        compiler_params=pltpu.CompilerParams(collective_id=0, has_side_effects=True, vmem_limit_bytes=54 * 2**20),
        cost_estimate=pl.CostEstimate(flops=10**9, bytes_accessed=16 * 2**20, transcendentals=0),
    )(row_v, row_u, col_u, col_v, diag, tile_u, tile_v, sketch)


def body(tile_u, tile_v, row_panel_u, row_panel_v, col_panel_u, col_panel_v, diag_inverse, sketch):
    w, tw, gram, cores, row_u, col_u = spread_panels(
        row_panel_v, row_panel_u, col_panel_u, col_panel_v, diag_inverse, tile_u[0], tile_v[0], sketch
    )
    new_u, new_v = recompress(tile_u[0], tile_v[0], row_u, col_u, cores, w, tw, gram)
    return new_u[None], new_v[None]


def solution(mesh):
    in_specs = (
        P("row", "col", None, None),
        P("row", "col", None, None),
        P("row", "col", None),
        P("row", "col", None),
        P("row", "col", None),
        P("row", "col", None),
        P("col", None),
        P(),
    )
    out_specs = (P("row", "col", None, None), P("row", "col", None, None))
    return jax.shard_map(body, mesh=mesh, in_specs=in_specs, out_specs=out_specs, check_vma=False)
```

```python
import math

import jax
import jax.numpy as jnp
from jax import lax
from jax.experimental import pallas as pl
from jax.experimental.pallas import tpu as pltpu
from jax.sharding import PartitionSpec as P

highest = lax.Precision.HIGHEST
f32, bf16 = jnp.float32, jnp.bfloat16
STEP = 2048


def halves(x):
    hi = x.astype(bf16)
    lo = (x - hi.astype(f32)).astype(bf16)
    return jnp.concatenate([hi, lo], axis=1)


def fold4(q):
    k = q.shape[0] // 2
    n = q.shape[1] // 2
    return q[:k, :n] + q[:k, n:] + q[k:, :n] + q[k:, n:]


def doubled(w):
    h = halves(w)
    return jnp.concatenate([h, h], axis=0)


def dot(a, b, ca=1, cb=0, precision=highest):
    return lax.dot_general(a, b, (((ca,), (cb,)), ((), ())), precision=precision, preferred_element_type=f32)


def dotb(a, b, ca=1, cb=0):
    return lax.dot_general(a, b, (((ca,), (cb,)), ((), ())), preferred_element_type=f32)


def split3(x):
    hi = x.astype(bf16).astype(f32)
    rest = x - hi
    mid = rest.astype(bf16).astype(f32)
    return hi, mid, rest - mid


def outer(a, b):
    ah, am, al = split3(a)
    bh, bm, bl = split3(b)
    left = jnp.concatenate([ah, am, ah, al, ah, am], axis=0).astype(bf16)
    right = jnp.concatenate([bh, bh, bm, bh, bl, bm], axis=0).astype(bf16)
    return dotb(left, right, 0, 0)


def inverse_factors(gram_ref, inv_ref, fac_ref):
    tiles, k, _ = gram_ref.shape
    row = lax.broadcasted_iota(jnp.int32, (tiles, 8, k), 1)
    lane = lax.broadcasted_iota(jnp.int32, (tiles, 8, k), 2)
    for p in range(k // 8):
        lo = 8 * p
        panel = gram_ref[:, lo : lo + 8, :]
        if p == 0:
            own = jnp.zeros((tiles, 8, k), f32)
        else:
            own = inv_ref[:, lo : lo + 8, :]
        own = own + jnp.where(lane == row + lo, 1.0, 0.0)
        cols = [jnp.broadcast_to(panel[:, :, lo + i : lo + i + 1], panel.shape) for i in range(8)]
        scale = jnp.zeros((tiles, 8, k), f32)
        pivot = jnp.zeros((tiles, 8, k), f32)
        for i in range(8):
            piv = jnp.broadcast_to(cols[i][:, i : i + 1, :], panel.shape)
            recip = 1.0 / piv
            scale = jnp.where(row == i, recip, scale)
            if i < 7:
                m = jnp.where(row > i, cols[i] * recip, 0.0)
                for j in range(i + 1, 8):
                    cols[j] = cols[j] - m * cols[j][:, i : i + 1, :]
                panel = panel - m * panel[:, i : i + 1, :]
                own = own - m * own[:, i : i + 1, :]
        fac_ref[:, lo : lo + 8, :] = own * jnp.sqrt(scale)
        if p < k // 8 - 1:
            lower = panel * scale
            for t in range(tiles):
                both = jnp.concatenate([panel[t], own[t]], axis=1)
                upd = outer(lower[t], both)
                gram_ref[t, lo + 8 :, :] = gram_ref[t, lo + 8 :, :] - upd[lo + 8 :, :k]
                if p == 0:
                    inv_ref[t, lo + 8 :, :] = -upd[lo + 8 :, k:]
                else:
                    inv_ref[t, lo + 8 :, :] = inv_ref[t, lo + 8 :, :] - upd[lo + 8 :, k:]


def finish_kernel(u_hbm, v_hbm, r_hbm, c_hbm, cores_hbm, w_hbm, t_hbm, gram_hbm, nu_hbm, nv_hbm,
                  ubuf, vbuf, cbuf, rbuf, uout, vout, cores_ref, w_ref, t_ref, gram_s, inv_s, fac_s, wide_s, in_sem, r_sem, out_sem):
    tiles, rows, k = uout.shape
    step = min(STEP, rows)
    scaling = math.sqrt(rows)

    def load(t, which):
        src, dst = ((u_hbm, ubuf), (v_hbm, vbuf), (c_hbm, cbuf))[which]
        return pltpu.make_async_copy(src.at[t], dst.at[t], in_sem.at[which, t])

    singles = [
        pltpu.make_async_copy(src, dst, r_sem.at[n])
        for n, (src, dst) in enumerate(((gram_hbm, gram_s), (w_hbm, w_ref), (t_hbm, t_ref), (cores_hbm, cores_ref), (r_hbm, rbuf)))
    ]
    for copy in singles:
        copy.start()
    for t in range(tiles):
        for which in range(3):
            load(t, which).start()
    singles[0].wait()
    inverse_factors(gram_s, inv_s, fac_s)

    def store(t, which):
        src, dst = ((uout, nu_hbm), (vout, nv_hbm))[which]
        return pltpu.make_async_copy(src.at[t], dst.at[t], out_sem.at[which, t])

    for copy in singles[1:]:
        copy.wait()
    for t in range(tiles):
        fac = fac_s[t]
        x = dot(w_ref[t], fac, 1, 1) * scaling
        y = dot(t_ref[t], fac, 1, 1) * (1.0 / scaling)
        c2 = -dot(cores_ref[t], y[k:], 0, 0)
        for n, part in enumerate((x[:k], x[k:], y[:k], c2)):
            wide_s[t, n] = doubled(part)
    for t in range(tiles):
        for which in range(3):
            load(t, which).wait()

        def finish(n, carry, t=t):
            at = pl.ds(pl.multiple_of(n * step, step), step)
            a = dotb(ubuf[t, at, :], wide_s[t, 0]) + dotb(rbuf[at, :], wide_s[t, 1])
            uout[t, at, :] = a[:, :k] + a[:, k:]
            b = dotb(vbuf[t, at, :], wide_s[t, 2]) + dotb(cbuf[t, at, :], wide_s[t, 3])
            vout[t, at, :] = b[:, :k] + b[:, k:]
            return carry

        lax.fori_loop(0, rows // step, finish, 0)
        store(t, 0).start()
        store(t, 1).start()
    for t in range(tiles):
        store(t, 0).wait()
        store(t, 1).wait()


def recompress(tile_u, tile_v, row_u, col_u, cores, w, tw, gram):
    tiles, rows, k = tile_u.shape[0], tile_u.shape[1], cores.shape[1]
    hbm = pl.BlockSpec(memory_space=pltpu.HBM)
    out = jax.ShapeDtypeStruct((tiles, rows, k), f32)
    return pl.pallas_call(
        finish_kernel,
        name="recompress",
        out_shape=(out, out),
        in_specs=[hbm] * 8,
        out_specs=(hbm, hbm),
        scratch_shapes=[
            pltpu.VMEM((tiles, rows, 2 * k), bf16),
            pltpu.VMEM((tiles, rows, 2 * k), bf16),
            pltpu.VMEM((tiles, rows, 2 * k), bf16),
            pltpu.VMEM((rows, 2 * k), bf16),
            pltpu.VMEM((tiles, rows, k), f32),
            pltpu.VMEM((tiles, rows, k), f32),
            pltpu.VMEM((tiles, k, k), f32),
            pltpu.VMEM((tiles, 2 * k, k), f32),
            pltpu.VMEM((tiles, 2 * k, k), f32),
            pltpu.VMEM((tiles, k, k), f32),
            pltpu.VMEM((tiles, k, k), f32),
            pltpu.VMEM((tiles, k, k), f32),
            pltpu.VMEM((tiles, 4, 2 * k, 2 * k), bf16),
            pltpu.SemaphoreType.DMA((3, tiles)),
            pltpu.SemaphoreType.DMA((5,)),
            pltpu.SemaphoreType.DMA((2, tiles)),
        ],
        compiler_params=pltpu.CompilerParams(vmem_limit_bytes=60 * 2**20),
        cost_estimate=pl.CostEstimate(flops=10**10, bytes_accessed=24 * 2**20, transcendentals=0),
    )(tile_u, tile_v, row_u, col_u, cores, w, tw, gram)


MESH = pl.DeviceIdType.MESH
CENTRE, ACROSS, LEFT, RIGHT = 0, 1, 0, 1


def mix(a, b):
    out = 0
    for bit in (4, 2, 1):
        out = out + bit * lax.rem(lax.div(a, bit) + lax.div(b, bit), 2)
    return out


class Links:
    def __init__(self, cols):
        self.r = lax.axis_index("row")
        self.c = lax.axis_index("col")
        self.cols = cols
        self.core = lax.rem(self.r, 2)
        self.m = lax.div(self.r, 2)
        self.x = lax.rem(self.m, 4)
        self.zl = lax.div(self.m, 4)
        self.mixed = mix(self.m, self.c)
        self.target = (2 * self.mixed + self.core, self.m)
        self.source = (2 * self.c + self.core, self.mixed)
        self.alone = jnp.logical_and(self.m == 0, self.c == 0)

    def chip(self, zl, x):
        return 4 * zl + x

    def at_chip(self, m):
        return (2 * m + self.core, self.c)


def remote(src, dst, send, recv, device):
    return pltpu.make_async_remote_copy(
        src_ref=src, dst_ref=dst, send_sem=send, recv_sem=recv, device_id=device, device_id_type=MESH
    )


class Spread:
    def __init__(self, at, src, buf, sems, w):
        self.at, self.src, self.buf, self.w = at, src, buf, w
        (self.t_send, self.t_recv, self.z_send, self.z_recv, self.x_send, self.x_recv,
         self.f_send, self.f_recv, self.d_send, self.d_recv, self.own_sem) = sems
        self.rows = src.shape[1]
        self.other = (at.r + 1 - 2 * at.core, at.c)
        xl, xr = lax.rem(at.x + 3, 4), lax.rem(at.x + 1, 4)
        self.xs = (xl, xr)
        self.far = lax.rem(at.x + 2, 4)
        self.zls = (at.zl, 1 - at.zl)

    def block(self, m, core=None, tile=None):
        core = self.at.core if core is None else core
        rows = pl.ds(pl.multiple_of(mix(m, self.at.c) * self.rows, self.rows), self.rows)
        if tile is None:
            return self.buf.at[pl.ds(2 * core, 2), rows, :]
        return self.buf.at[pl.ds(2 * core + tile, 1), rows, :]

    def transpose_copy(self):
        at = self.at
        rows = pl.ds(pl.multiple_of(at.c * self.rows, self.rows), self.rows)
        dst = self.buf.at[pl.ds(2 * at.core, 2), rows, :]
        return remote(self.src, dst, self.t_send.at[self.w], self.t_recv.at[self.w], at.target)

    def transpose_local(self):
        return pltpu.make_async_copy(self.src, self.block(self.at.m), self.own_sem.at[self.w])

    def transpose_start(self):
        @pl.when(jnp.logical_not(self.at.alone))
        def _():
            self.transpose_copy().start()

        @pl.when(self.at.alone)
        def _():
            self.transpose_local().start()

    def transpose_wait(self):
        at = self.at

        @pl.when(jnp.logical_not(at.alone))
        def _():
            own = self.block(at.m)
            remote(own, own, self.t_send.at[self.w], self.t_recv.at[self.w], at.source).wait_recv()

        @pl.when(at.alone)
        def _():
            self.transpose_local().wait()

    def z_copy(self, zl):
        b = self.block(self.at.chip(zl, self.at.x))
        return remote(b, b, self.z_send.at[self.w], self.z_recv.at[self.w], self.at.at_chip(self.at.chip(self.zls[1], self.at.x)))

    def x_copy(self, s, to):
        b = self.block(self.at.chip(self.zls[s], self.at.x))
        return remote(b, b, self.x_send.at[self.w, s, to], self.x_recv.at[self.w, s, 1 - to], self.at.at_chip(self.at.chip(self.at.zl, self.xs[to])))

    def x_wait(self, s, came):
        b = self.block(self.at.chip(self.zls[s], self.xs[came]))
        remote(b, b, self.x_send.at[self.w, s, came], self.x_recv.at[self.w, s, came], self.other).wait_recv()

    def f_copy(self, s, came):
        b = self.block(self.at.chip(self.zls[s], self.xs[came]), tile=came)
        return remote(b, b, self.f_send.at[self.w, s, came], self.f_recv.at[self.w, s, came], self.at.at_chip(self.at.chip(self.at.zl, self.xs[1 - came])))

    def f_wait(self, s, came):
        b = self.block(self.at.chip(self.zls[s], self.far), tile=came)
        remote(b, b, self.f_send.at[self.w, s, came], self.f_recv.at[self.w, s, came], self.other).wait_recv()

    def d_copy(self, n, core=None):
        at = self.at
        core = at.core if core is None else core
        if n < 2:
            b = self.block(at.chip(self.zls[n], at.x), core)
        elif n < 6:
            s, came = divmod(n - 2, 2)
            b = self.block(at.chip(self.zls[s], self.xs[came]), core)
        else:
            s, came = divmod(n - 6, 2)
            b = self.block(at.chip(self.zls[s], self.far), core, came)
        return remote(b, b, self.d_send.at[self.w, n], self.d_recv.at[self.w, n], self.other)

    def stage_own(self):
        self.transpose_wait()
        self.x_copy(0, LEFT).start()
        self.x_copy(0, RIGHT).start()
        self.z_copy(self.zls[0]).start()
        self.d_copy(0).start()

    def stage_partner(self):
        self.z_copy(self.zls[1]).wait_recv()
        self.x_copy(1, LEFT).start()
        self.x_copy(1, RIGHT).start()
        self.d_copy(1).start()

    def stage_forward(self, s):
        for came in (LEFT, RIGHT):
            self.x_wait(s, came)
            self.f_copy(s, came).start()
            self.d_copy(2 + 2 * s + came).start()

    def stage_far(self, s):
        for came in (LEFT, RIGHT):
            self.f_wait(s, came)
            self.d_copy(6 + 2 * s + came).start()

    def stage_other_core(self):
        for n in range(10):
            self.d_copy(n, 1 - self.at.core).wait_recv()

    def drain(self):
        @pl.when(jnp.logical_not(self.at.alone))
        def _():
            self.transpose_copy().wait_send()

        self.z_copy(self.zls[0]).wait_send()
        for s in (0, 1):
            for to in (LEFT, RIGHT):
                self.x_copy(s, to).wait_send()
                self.f_copy(s, to).wait_send()
        for n in range(10):
            self.d_copy(n).wait_send()


def greet(at, before_wait):
    barrier = pltpu.get_barrier_semaphore()

    def hello(device):
        pl.semaphore_signal(barrier, inc=1, device_id=device, device_id_type=MESH)

    for step in range(1, at.cols):
        hello((at.r, lax.rem(at.c + step, at.cols)))
    hello((at.r + 1 - 2 * at.core, at.c))
    hello(at.at_chip(at.chip(1 - at.zl, at.x)))
    hello(at.at_chip(at.chip(at.zl, lax.rem(at.x + 1, 4))))
    hello(at.at_chip(at.chip(at.zl, lax.rem(at.x + 3, 4))))

    @pl.when(jnp.logical_not(at.alone))
    def _():
        hello(at.target)
        hello(at.source)

    before_wait()

    @pl.when(jnp.logical_not(at.alone))
    def _():
        pl.semaphore_wait(barrier, at.cols + 5)

    @pl.when(at.alone)
    def _():
        pl.semaphore_wait(barrier, at.cols + 3)


class Group:
    def __init__(self, at, send, recv):
        self.at, self.send, self.recv = at, send, recv

    def copy(self, src, dst, to):
        return remote(src, dst, self.send.at[to], self.recv.at[self.at.c], (self.at.r, to))

    def wait_from(self, dst, source):
        remote(dst, dst, self.send.at[source], self.recv.at[source], (self.at.r, source)).wait_recv()


class Tree:
    def __init__(self, at, block, sems):
        self.at, self.block = at, block
        self.z_send, self.z_recv, self.y_send, self.y_recv, self.f_send, self.f_recv = sems
        y, zh = lax.div(at.c, 2), lax.rem(at.c, 2)
        self.zhs = (zh, 1 - zh)
        self.ys = (lax.rem(y + 3, 4), lax.rem(y + 1, 4))
        self.y, self.far = y, lax.rem(y + 2, 4)

    def col(self, y, s):
        return 2 * y + self.zhs[s]

    def z_copy(self, s):
        b = self.block(self.col(self.y, s))
        return remote(b, b, self.z_send.at[0], self.z_recv.at[0], (self.at.r, self.col(self.y, 1)))

    def y_copy(self, s, to):
        b = self.block(self.col(self.y, s))
        return remote(b, b, self.y_send.at[s, to], self.y_recv.at[s, 1 - to], (self.at.r, self.col(self.ys[to], 0)))

    def y_wait(self, s, came):
        b = self.block(self.col(self.ys[came], s))
        remote(b, b, self.y_send.at[s, came], self.y_recv.at[s, came], (self.at.r, self.col(self.ys[came], 0))).wait_recv()

    def f_copy(self, s, came):
        b = self.block(self.col(self.ys[came], s), came)
        return remote(b, b, self.f_send.at[s, came], self.f_recv.at[s, came], (self.at.r, self.col(self.ys[1 - came], 0)))

    def f_wait(self, s, came):
        b = self.block(self.col(self.far, s), came)
        remote(b, b, self.f_send.at[s, came], self.f_recv.at[s, came], (self.at.r, self.col(self.ys[came], 0))).wait_recv()

    def stage_own(self):
        self.z_copy(0).start()
        self.y_copy(0, LEFT).start()
        self.y_copy(0, RIGHT).start()

    def stage_partner(self):
        self.z_copy(1).wait_recv()
        self.y_copy(1, LEFT).start()
        self.y_copy(1, RIGHT).start()

    def stage_forward(self, s):
        for came in (LEFT, RIGHT):
            self.y_wait(s, came)
            self.f_copy(s, came).start()

    def stage_far(self, s):
        for came in (LEFT, RIGHT):
            self.f_wait(s, came)

    def drain(self):
        self.z_copy(0).wait_send()
        for s in (0, 1):
            for to in (LEFT, RIGHT):
                self.y_copy(s, to).wait_send()
                self.f_copy(s, to).wait_send()


def panel_kernel(rv_hbm, ru_hbm, cu_hbm, cv_hbm, d_hbm, u_hbm, v_hbm, s_ref, w_ref, t_ref, gram_ref, cores_ref, rs_hbm, us_hbm, vs_hbm, cs_hbm,
                 vblk, vsp, rbuf, rsp, dbuf, dsp, zpart, zsend, zt, zsp, cub, cvb, csp, xsp, ubuf, vbuf, usp, wsp, tts, ttr, uu_s, p1_s, p2_s, ru_s,
                 v_send, v_recv, p_send, p_recv, rz_send, rz_recv, ry_send, ry_recv, rf_send, rf_recv,
                 qz_send, qz_recv, qy_send, qy_recv, qf_send, qf_recv,
                 t_send, t_recv, z_send, z_recv, x_send, x_recv, f_send, f_recv, d_send, d_recv, own_sem, in_sem, out_sem, uv_sem, save_sem):
    cols, part, k = vblk.shape
    tiles = ubuf.shape[0]
    rows = cols * part
    at = Links(cols)
    sems = (t_send, t_recv, z_send, z_recv, x_send, x_recv, f_send, f_recv, d_send, d_recv, own_sem)
    cv = Spread(at, cv_hbm, cvb, sems, 0)
    cu = Spread(at, cu_hbm, cub, sems, 1)
    vg, pg = Group(at, v_send, v_recv), Group(at, p_send, p_recv)

    def span(b):
        return pl.ds(pl.multiple_of(b * part, part), part)

    def rblock(b, half=None):
        if half is None:
            return rbuf.at[span(b), :]
        size = part // 2
        return rbuf.at[pl.ds(pl.multiple_of(b * part + half * size, size), size), :]

    def zblock(b, half=None):
        if half is None:
            return zt.at[b]
        size = k // 2
        return zt.at[b, size * half : size * (half + 1), :]

    rg = Tree(at, rblock, (rz_send, rz_recv, ry_send, ry_recv, rf_send, rf_recv))
    qg = Tree(at, zblock, (qz_send, qz_recv, qy_send, qy_recv, qf_send, qf_recv))

    def others(do, keep=None):
        for step in range(1, cols):
            b = lax.rem(at.c + step, cols)
            if keep is None:
                do(b)
            else:

                @pl.when(keep(b))
                def _(b=b):
                    do(b)

    later, earlier = (lambda b: b > at.c), (lambda b: b < at.c)
    load_d = pltpu.make_async_copy(d_hbm, dbuf, in_sem.at[0])
    load_v = pltpu.make_async_copy(rv_hbm.at[0], vblk.at[at.c], in_sem.at[1])
    load_r = pltpu.make_async_copy(ru_hbm.at[0], rblock(at.c), in_sem.at[2])

    def load_tile(t, which):
        src, dst = ((u_hbm, ubuf), (v_hbm, vbuf))[which]
        return pltpu.make_async_copy(src.at[t], dst.at[t], uv_sem.at[which, t])

    def save(n, t):
        src, dst = ((usp, us_hbm), (wsp, vs_hbm), (csp, cs_hbm))[n]
        return pltpu.make_async_copy(src.at[t], dst.at[t], save_sem.at[n, t])

    load_d.start()
    load_v.start()
    load_r.start()

    def split_d(b, carry):
        d = dbuf[:, span(b)]
        hi = d.astype(bf16)
        dsp[0, :, span(b)] = hi
        dsp[1, :, span(b)] = (d - hi.astype(f32)).astype(bf16)
        return carry

    def prepare():
        for b in range(cols):

            @pl.when(b > at.c)
            def _(b=b):
                vsp[part * b : part * (b + 1), :] = jnp.zeros((part, 2 * k), bf16)

        load_v.wait()
        vsp[span(at.c), :] = halves(vblk[at.c])
        load_d.wait()
        lax.fori_loop(0, cols, split_d, 0)

    greet(at, prepare)
    others(lambda b: vg.copy(rv_hbm.at[0], vblk.at[at.c], b).start(), later)
    cv.transpose_start()
    cu.transpose_start()
    for t in range(tiles):
        load_tile(t, 0).start()
        load_tile(t, 1).start()

    def split_s(b, carry):
        tts[:, span(b)] = halves(s_ref[span(b), :]).astype(f32).T.astype(bf16)
        return carry

    lax.fori_loop(0, cols, split_s, 0)

    def split_into(dst, src):
        def body(b, carry):
            dst[span(b), :] = halves(src[span(b), :])
            return carry

        lax.fori_loop(0, cols, body, 0)

    def split_all(dst, src):
        def body(b, carry):
            for t in range(tiles):
                dst[t, span(b), :] = halves(src[t, span(b), :])
            return carry

        lax.fori_loop(0, cols, body, 0)

    def tile_products(t):
        load_tile(t, 0).wait()
        load_tile(t, 1).wait()
        split_into(usp.at[t], ubuf.at[t])
        split_into(wsp.at[t], vbuf.at[t])
        save(0, t).start()
        save(1, t).start()
        uu_s[t] = fold4(dotb(usp[t], usp[t], 0, 0))
        p1_s[t] = fold4(dotb(tts[...], wsp[t]))

    cv.stage_own()
    cu.stage_own()

    def arrived(b, carry):
        vg.wait_from(vblk.at[b], b)
        vsp[span(b), :] = halves(vblk[b])
        return carry

    lax.fori_loop(0, at.c, arrived, 0)
    q = dotb(dsp[0], vsp[...]) + dotb(dsp[1], vsp[...])
    yt = halves(q[:, :k] + q[:, k:]).astype(f32).T.astype(bf16)
    for b in range(cols):
        q = dotb(yt, dsp[0, :, part * b : part * (b + 1)]) + dotb(yt, dsp[1, :, part * b : part * (b + 1)])
        zsend[b] = q[:k] + q[k:]
    others(lambda b: pg.copy(zsend.at[b], zpart.at[at.c], b).start(), earlier)
    cv.stage_partner()
    cu.stage_partner()
    load_r.wait()
    rg.stage_own()
    tile_products(0)
    cv.stage_forward(0)
    zt[at.c] = zsend[at.c]

    def gather(n, carry):
        b = cols - 1 - n
        pg.wait_from(zpart.at[b], b)
        zt[at.c] = zt[at.c] + zpart[b]
        return carry

    lax.fori_loop(0, cols - 1 - at.c, gather, 0)
    qg.stage_own()
    cv.stage_forward(1)
    rg.stage_partner()
    tile_products(1)
    qg.stage_partner()
    cu.stage_forward(0)
    rg.stage_forward(0)
    qg.stage_forward(0)
    cv.stage_far(0)
    cv.stage_far(1)
    tile_products(2)
    rg.stage_forward(1)
    qg.stage_forward(1)
    cu.stage_forward(1)
    tile_products(3)
    rg.stage_far(0)
    rg.stage_far(1)

    def split_r(b, carry):
        h = halves(rbuf[span(b), :])
        rsp[span(b), :] = h
        ttr[:, span(b)] = h.astype(f32).T.astype(bf16)
        return carry

    lax.fori_loop(0, cols, split_r, 0)
    out_r = pltpu.make_async_copy(rsp, rs_hbm, out_sem.at[0])
    out_r.start()
    rr = fold4(dotb(ttr[...], rsp[...]))
    for t in range(tiles):
        ru_s[t] = fold4(dotb(ttr[...], usp[t]))
    cv.stage_other_core()
    cu.stage_far(0)
    cu.stage_far(1)
    split_all(xsp, cvb)
    qg.stage_far(0)
    qg.stage_far(1)
    for b in range(cols):
        z = zt[b]
        hi = z.astype(bf16)
        zsp[:k, part * b : part * (b + 1)] = hi
        zsp[k:, part * b : part * (b + 1)] = (z - hi.astype(f32)).astype(bf16)
    for t in range(tiles):
        cores_ref[t] = fold4(dotb(zsp[...], xsp[t]))
    cu.stage_other_core()
    split_all(csp, cub)
    for t in range(tiles):
        save(2, t).start()
    for t in range(tiles):
        p2_s[t] = fold4(dotb(tts[...], csp[t]))
    ws = []
    for t in range(tiles):
        w2 = -dot(cores_ref[t], p2_s[t], 1, 1)
        ws.append(jnp.concatenate([p1_s[t].T, w2], axis=0))
        w_ref[t] = ws[t]
    tws = []
    for t in range(tiles):
        ru = ru_s[t]
        g = jnp.concatenate([jnp.concatenate([uu_s[t], ru.T], axis=1), jnp.concatenate([ru, rr], axis=1)], axis=0)
        tws.append(dot(g, ws[t]))
        t_ref[t] = tws[t]
    for t in range(tiles):
        gram_ref[t] = dot(ws[t], tws[t], 0, 0)

    others(lambda b: vg.copy(rv_hbm.at[0], vblk.at[at.c], b).wait_send(), later)
    others(lambda b: pg.copy(zsend.at[b], zpart.at[at.c], b).wait_send(), earlier)
    rg.drain()
    qg.drain()
    cv.drain()
    cu.drain()
    out_r.wait()
    for t in range(tiles):
        for n in range(3):
            save(n, t).wait()


def spread_panels(row_v, row_u, col_u, col_v, diag, tile_u, tile_v, sketch):
    cols = lax.axis_size("col")
    tiles = tile_u.shape[0]
    part, k = row_v.shape[1:]
    rows = cols * part
    vm = pl.BlockSpec(memory_space=pltpu.VMEM)
    hbm = pl.BlockSpec(memory_space=pltpu.HBM)
    dma = pltpu.SemaphoreType.DMA
    return pl.pallas_call(
        panel_kernel,
        name="spread_panels",
        out_shape=(
            jax.ShapeDtypeStruct((tiles, 2 * k, k), f32),
            jax.ShapeDtypeStruct((tiles, 2 * k, k), f32),
            jax.ShapeDtypeStruct((tiles, k, k), f32),
            jax.ShapeDtypeStruct((tiles, k, k), f32),
            jax.ShapeDtypeStruct((rows, 2 * k), bf16),
            jax.ShapeDtypeStruct((tiles, rows, 2 * k), bf16),
            jax.ShapeDtypeStruct((tiles, rows, 2 * k), bf16),
            jax.ShapeDtypeStruct((tiles, rows, 2 * k), bf16),
        ),
        in_specs=[hbm] * 7 + [vm],
        out_specs=(vm, vm, vm, vm, hbm, hbm, hbm, hbm),
        scratch_shapes=[
            pltpu.VMEM((cols, part, k), f32),
            pltpu.VMEM((rows, 2 * k), bf16),
            pltpu.VMEM((rows, k), f32),
            pltpu.VMEM((rows, 2 * k), bf16),
            pltpu.VMEM((part, rows), f32),
            pltpu.VMEM((2, part, rows), bf16),
            pltpu.VMEM((cols, k, part), f32),
            pltpu.VMEM((cols, k, part), f32),
            pltpu.VMEM((cols, k, part), f32),
            pltpu.VMEM((2 * k, rows), bf16),
            pltpu.VMEM((tiles, rows, k), f32),
            pltpu.VMEM((tiles, rows, k), f32),
            pltpu.VMEM((tiles, rows, 2 * k), bf16),
            pltpu.VMEM((tiles, rows, 2 * k), bf16),
            pltpu.VMEM((tiles, rows, k), f32),
            pltpu.VMEM((tiles, rows, k), f32),
            pltpu.VMEM((tiles, rows, 2 * k), bf16),
            pltpu.VMEM((tiles, rows, 2 * k), bf16),
            pltpu.VMEM((2 * k, rows), bf16),
            pltpu.VMEM((2 * k, rows), bf16),
            pltpu.VMEM((tiles, k, k), f32),
            pltpu.VMEM((tiles, k, k), f32),
            pltpu.VMEM((tiles, k, k), f32),
            pltpu.VMEM((tiles, k, k), f32),
        ]
        + [dma((cols,))] * 4
        + ([dma((1,))] * 2 + [dma((2, 2))] * 4) * 2
        + [dma((2,))] * 4
        + [dma((2, 2, 2))] * 4
        + [dma((2, 10))] * 2
        + [dma((2,)), dma((3,)), dma((1,)), dma((2, tiles)), dma((3, tiles))],
        compiler_params=pltpu.CompilerParams(collective_id=0, has_side_effects=True, vmem_limit_bytes=54 * 2**20),
        cost_estimate=pl.CostEstimate(flops=10**9, bytes_accessed=16 * 2**20, transcendentals=0),
    )(row_v, row_u, col_u, col_v, diag, tile_u, tile_v, sketch)


def body(tile_u, tile_v, row_panel_u, row_panel_v, col_panel_u, col_panel_v, diag_inverse, sketch):
    w, tw, gram, cores, row_u, split_u, split_v, col_u = spread_panels(
        row_panel_v, row_panel_u, col_panel_u, col_panel_v, diag_inverse, tile_u[0], tile_v[0], sketch
    )
    new_u, new_v = recompress(split_u, split_v, row_u, col_u, cores, w, tw, gram)
    return new_u[None], new_v[None]


def solution(mesh):
    in_specs = (
        P("row", "col", None, None),
        P("row", "col", None, None),
        P("row", "col", None),
        P("row", "col", None),
        P("row", "col", None),
        P("row", "col", None),
        P("col", None),
        P(),
    )
    out_specs = (P("row", "col", None, None), P("row", "col", None, None))
    return jax.shard_map(body, mesh=mesh, in_specs=in_specs, out_specs=out_specs, check_vma=False)
```

```python
import math

import jax
import jax.numpy as jnp
from jax import lax
from jax.experimental import pallas as pl
from jax.experimental.pallas import tpu as pltpu
from jax.sharding import PartitionSpec as P

highest = lax.Precision.HIGHEST
f32, bf16 = jnp.float32, jnp.bfloat16
STEP = 2048


def halves(x):
    hi = x.astype(bf16)
    lo = (x - hi.astype(f32)).astype(bf16)
    return jnp.concatenate([hi, lo], axis=1)


def fold4(q):
    k = q.shape[0] // 2
    n = q.shape[1] // 2
    return q[:k, :n] + q[:k, n:] + q[k:, :n] + q[k:, n:]


def doubled(w):
    h = halves(w)
    return jnp.concatenate([h, h], axis=0)


def dot(a, b, ca=1, cb=0, precision=highest):
    return lax.dot_general(a, b, (((ca,), (cb,)), ((), ())), precision=precision, preferred_element_type=f32)


def dotb(a, b, ca=1, cb=0):
    return lax.dot_general(a, b, (((ca,), (cb,)), ((), ())), preferred_element_type=f32)


def split3(x):
    hi = x.astype(bf16).astype(f32)
    rest = x - hi
    mid = rest.astype(bf16).astype(f32)
    return hi, mid, rest - mid


def outer(a, b):
    ah, am, al = split3(a)
    bh, bm, bl = split3(b)
    left = jnp.concatenate([ah, am, ah, al, ah, am], axis=0).astype(bf16)
    right = jnp.concatenate([bh, bh, bm, bh, bl, bm], axis=0).astype(bf16)
    return dotb(left, right, 0, 0)


def inverse_factors(gram_ref, inv_ref, fac_ref):
    tiles, k, _ = gram_ref.shape
    row = lax.broadcasted_iota(jnp.int32, (tiles, 8, k), 1)
    lane = lax.broadcasted_iota(jnp.int32, (tiles, 8, k), 2)
    for p in range(k // 8):
        lo = 8 * p
        panel = gram_ref[:, lo : lo + 8, :]
        if p == 0:
            own = jnp.zeros((tiles, 8, k), f32)
        else:
            own = inv_ref[:, lo : lo + 8, :]
        own = own + jnp.where(lane == row + lo, 1.0, 0.0)
        cols = [jnp.broadcast_to(panel[:, :, lo + i : lo + i + 1], panel.shape) for i in range(8)]
        scale = jnp.zeros((tiles, 8, k), f32)
        pivot = jnp.zeros((tiles, 8, k), f32)
        for i in range(8):
            piv = jnp.broadcast_to(cols[i][:, i : i + 1, :], panel.shape)
            recip = 1.0 / piv
            scale = jnp.where(row == i, recip, scale)
            if i < 7:
                m = jnp.where(row > i, cols[i] * recip, 0.0)
                for j in range(i + 1, 8):
                    cols[j] = cols[j] - m * cols[j][:, i : i + 1, :]
                panel = panel - m * panel[:, i : i + 1, :]
                own = own - m * own[:, i : i + 1, :]
        fac_ref[:, lo : lo + 8, :] = own * jnp.sqrt(scale)
        if p < k // 8 - 1:
            lower = panel * scale
            for t in range(tiles):
                both = jnp.concatenate([panel[t], own[t]], axis=1)
                upd = outer(lower[t], both)
                gram_ref[t, lo + 8 :, :] = gram_ref[t, lo + 8 :, :] - upd[lo + 8 :, :k]
                if p == 0:
                    inv_ref[t, lo + 8 :, :] = -upd[lo + 8 :, k:]
                else:
                    inv_ref[t, lo + 8 :, :] = inv_ref[t, lo + 8 :, :] - upd[lo + 8 :, k:]


def finish_kernel(u_hbm, v_hbm, r_hbm, c_hbm, cores_hbm, w_hbm, t_hbm, gram_hbm, nu_hbm, nv_hbm,
                  ubuf, vbuf, cbuf, rbuf, uout, vout, cores_ref, w_ref, t_ref, gram_s, inv_s, fac_s, wide_s, in_sem, r_sem, out_sem):
    tiles, rows, k = uout.shape
    step = min(STEP, rows)
    scaling = math.sqrt(rows)

    def load(t, which):
        src, dst = ((u_hbm, ubuf), (v_hbm, vbuf), (c_hbm, cbuf))[which]
        return pltpu.make_async_copy(src.at[t], dst.at[t], in_sem.at[which, t])

    singles = [
        pltpu.make_async_copy(src, dst, r_sem.at[n])
        for n, (src, dst) in enumerate(((gram_hbm, gram_s), (w_hbm, w_ref), (t_hbm, t_ref), (cores_hbm, cores_ref), (r_hbm, rbuf)))
    ]
    for copy in singles:
        copy.start()
    for t in range(tiles):
        for which in range(3):
            load(t, which).start()
    singles[0].wait()
    inverse_factors(gram_s, inv_s, fac_s)

    def store(t, which):
        src, dst = ((uout, nu_hbm), (vout, nv_hbm))[which]
        return pltpu.make_async_copy(src.at[t], dst.at[t], out_sem.at[which, t])

    for copy in singles[1:]:
        copy.wait()
    for t in range(tiles):
        fac = fac_s[t]
        x = dot(w_ref[t], fac, 1, 1) * scaling
        y = dot(t_ref[t], fac, 1, 1) * (1.0 / scaling)
        c2 = -dot(cores_ref[t], y[k:], 0, 0)
        for n, part in enumerate((x[:k], x[k:], y[:k], c2)):
            wide_s[t, n] = doubled(part)
    for t in range(tiles):
        for which in range(3):
            load(t, which).wait()

        def finish(n, carry, t=t):
            at = pl.ds(pl.multiple_of(n * step, step), step)
            a = dotb(ubuf[t, at, :], wide_s[t, 0]) + dotb(rbuf[at, :], wide_s[t, 1])
            uout[t, at, :] = a[:, :k] + a[:, k:]
            b = dotb(vbuf[t, at, :], wide_s[t, 2]) + dotb(cbuf[t, at, :], wide_s[t, 3])
            vout[t, at, :] = b[:, :k] + b[:, k:]
            return carry

        lax.fori_loop(0, rows // step, finish, 0)
        store(t, 0).start()
        store(t, 1).start()
    for t in range(tiles):
        store(t, 0).wait()
        store(t, 1).wait()


def recompress(tile_u, tile_v, row_u, col_u, cores, w, tw, gram):
    tiles, rows, k = tile_u.shape[0], tile_u.shape[1], cores.shape[1]
    hbm = pl.BlockSpec(memory_space=pltpu.HBM)
    out = jax.ShapeDtypeStruct((tiles, rows, k), f32)
    return pl.pallas_call(
        finish_kernel,
        name="recompress",
        out_shape=(out, out),
        in_specs=[hbm] * 8,
        out_specs=(hbm, hbm),
        scratch_shapes=[
            pltpu.VMEM((tiles, rows, 2 * k), bf16),
            pltpu.VMEM((tiles, rows, 2 * k), bf16),
            pltpu.VMEM((tiles, rows, 2 * k), bf16),
            pltpu.VMEM((rows, 2 * k), bf16),
            pltpu.VMEM((tiles, rows, k), f32),
            pltpu.VMEM((tiles, rows, k), f32),
            pltpu.VMEM((tiles, k, k), f32),
            pltpu.VMEM((tiles, 2 * k, k), f32),
            pltpu.VMEM((tiles, 2 * k, k), f32),
            pltpu.VMEM((tiles, k, k), f32),
            pltpu.VMEM((tiles, k, k), f32),
            pltpu.VMEM((tiles, k, k), f32),
            pltpu.VMEM((tiles, 4, 2 * k, 2 * k), bf16),
            pltpu.SemaphoreType.DMA((3, tiles)),
            pltpu.SemaphoreType.DMA((5,)),
            pltpu.SemaphoreType.DMA((2, tiles)),
        ],
        compiler_params=pltpu.CompilerParams(vmem_limit_bytes=60 * 2**20),
        cost_estimate=pl.CostEstimate(flops=10**10, bytes_accessed=24 * 2**20, transcendentals=0),
    )(tile_u, tile_v, row_u, col_u, cores, w, tw, gram)


MESH = pl.DeviceIdType.MESH
CENTRE, ACROSS, LEFT, RIGHT = 0, 1, 0, 1


def mix(a, b):
    out = 0
    for bit in (4, 2, 1):
        out = out + bit * lax.rem(lax.div(a, bit) + lax.div(b, bit), 2)
    return out


class Links:
    def __init__(self, cols):
        self.r = lax.axis_index("row")
        self.c = lax.axis_index("col")
        self.cols = cols
        self.core = lax.rem(self.r, 2)
        self.m = lax.div(self.r, 2)
        self.x = lax.rem(self.m, 4)
        self.zl = lax.div(self.m, 4)
        self.turn = 6 * self.core
        self.mixed = mix(mix(self.m, self.c), self.turn)
        self.target = (2 * self.mixed + self.core, self.m)
        self.source = (2 * self.c + self.core, self.mixed)
        self.alone = jnp.logical_and(self.m == self.c, self.c == self.turn)

    def chip(self, zl, x):
        return 4 * zl + x

    def at_chip(self, m):
        return (2 * m + self.core, self.c)


def remote(src, dst, send, recv, device):
    return pltpu.make_async_remote_copy(
        src_ref=src, dst_ref=dst, send_sem=send, recv_sem=recv, device_id=device, device_id_type=MESH
    )


class Spread:
    def __init__(self, at, src, buf, sems, w):
        self.at, self.src, self.buf, self.w = at, src, buf, w
        (self.t_send, self.t_recv, self.z_send, self.z_recv, self.x_send, self.x_recv,
         self.f_send, self.f_recv, self.d_send, self.d_recv, self.own_sem) = sems
        self.rows = src.shape[1]
        self.other = (at.r + 1 - 2 * at.core, at.c)
        xl, xr = lax.rem(at.x + 3, 4), lax.rem(at.x + 1, 4)
        self.xs = (xl, xr)
        self.far = lax.rem(at.x + 2, 4)
        self.zls = (at.zl, 1 - at.zl)

    def block(self, m, core=None, tile=None):
        core = self.at.core if core is None else core
        rows = pl.ds(pl.multiple_of(mix(mix(m, self.at.c), 6 * core) * self.rows, self.rows), self.rows)
        if tile is None:
            return self.buf.at[pl.ds(2 * core, 2), rows, :]
        return self.buf.at[pl.ds(2 * core + tile, 1), rows, :]

    def transpose_copy(self):
        at = self.at
        rows = pl.ds(pl.multiple_of(at.c * self.rows, self.rows), self.rows)
        dst = self.buf.at[pl.ds(2 * at.core, 2), rows, :]
        return remote(self.src, dst, self.t_send.at[self.w], self.t_recv.at[self.w], at.target)

    def transpose_local(self):
        return pltpu.make_async_copy(self.src, self.block(self.at.m), self.own_sem.at[self.w])

    def transpose_start(self):
        @pl.when(jnp.logical_not(self.at.alone))
        def _():
            self.transpose_copy().start()

        @pl.when(self.at.alone)
        def _():
            self.transpose_local().start()

    def transpose_wait(self):
        at = self.at

        @pl.when(jnp.logical_not(at.alone))
        def _():
            own = self.block(at.m)
            remote(own, own, self.t_send.at[self.w], self.t_recv.at[self.w], at.source).wait_recv()

        @pl.when(at.alone)
        def _():
            self.transpose_local().wait()

    def z_copy(self, zl):
        b = self.block(self.at.chip(zl, self.at.x))
        return remote(b, b, self.z_send.at[self.w], self.z_recv.at[self.w], self.at.at_chip(self.at.chip(self.zls[1], self.at.x)))

    def x_copy(self, s, to):
        b = self.block(self.at.chip(self.zls[s], self.at.x))
        return remote(b, b, self.x_send.at[self.w, s, to], self.x_recv.at[self.w, s, 1 - to], self.at.at_chip(self.at.chip(self.at.zl, self.xs[to])))

    def x_wait(self, s, came):
        b = self.block(self.at.chip(self.zls[s], self.xs[came]))
        remote(b, b, self.x_send.at[self.w, s, came], self.x_recv.at[self.w, s, came], self.other).wait_recv()

    def f_copy(self, s, came):
        b = self.block(self.at.chip(self.zls[s], self.xs[came]), tile=came)
        return remote(b, b, self.f_send.at[self.w, s, came], self.f_recv.at[self.w, s, came], self.at.at_chip(self.at.chip(self.at.zl, self.xs[1 - came])))

    def f_wait(self, s, came):
        b = self.block(self.at.chip(self.zls[s], self.far), tile=came)
        remote(b, b, self.f_send.at[self.w, s, came], self.f_recv.at[self.w, s, came], self.other).wait_recv()

    def d_copy(self, n, core=None):
        at = self.at
        core = at.core if core is None else core
        if n < 2:
            b = self.block(at.chip(self.zls[n], at.x), core)
        elif n < 6:
            s, came = divmod(n - 2, 2)
            b = self.block(at.chip(self.zls[s], self.xs[came]), core)
        else:
            s, came = divmod(n - 6, 2)
            b = self.block(at.chip(self.zls[s], self.far), core, came)
        return remote(b, b, self.d_send.at[self.w, n], self.d_recv.at[self.w, n], self.other)

    def stage_own(self):
        self.transpose_wait()
        self.x_copy(0, LEFT).start()
        self.x_copy(0, RIGHT).start()
        self.z_copy(self.zls[0]).start()
        self.d_copy(0).start()

    def stage_partner(self):
        self.z_copy(self.zls[1]).wait_recv()
        self.x_copy(1, LEFT).start()
        self.x_copy(1, RIGHT).start()
        self.d_copy(1).start()

    def stage_forward(self, s):
        for came in (LEFT, RIGHT):
            self.x_wait(s, came)
            self.f_copy(s, came).start()
            self.d_copy(2 + 2 * s + came).start()

    def stage_far(self, s):
        for came in (LEFT, RIGHT):
            self.f_wait(s, came)
            self.d_copy(6 + 2 * s + came).start()

    def stage_other_core(self):
        for n in range(10):
            self.d_copy(n, 1 - self.at.core).wait_recv()

    def drain(self):
        @pl.when(jnp.logical_not(self.at.alone))
        def _():
            self.transpose_copy().wait_send()

        self.z_copy(self.zls[0]).wait_send()
        for s in (0, 1):
            for to in (LEFT, RIGHT):
                self.x_copy(s, to).wait_send()
                self.f_copy(s, to).wait_send()
        for n in range(10):
            self.d_copy(n).wait_send()


def greet(at, before_wait):
    barrier = pltpu.get_barrier_semaphore()

    def hello(device):
        pl.semaphore_signal(barrier, inc=1, device_id=device, device_id_type=MESH)

    for step in range(1, at.cols):
        hello((at.r, lax.rem(at.c + step, at.cols)))
    hello((at.r + 1 - 2 * at.core, at.c))
    hello(at.at_chip(at.chip(1 - at.zl, at.x)))
    hello(at.at_chip(at.chip(at.zl, lax.rem(at.x + 1, 4))))
    hello(at.at_chip(at.chip(at.zl, lax.rem(at.x + 3, 4))))

    @pl.when(jnp.logical_not(at.alone))
    def _():
        hello(at.target)
        hello(at.source)

    before_wait()

    @pl.when(jnp.logical_not(at.alone))
    def _():
        pl.semaphore_wait(barrier, at.cols + 5)

    @pl.when(at.alone)
    def _():
        pl.semaphore_wait(barrier, at.cols + 3)


class Group:
    def __init__(self, at, send, recv):
        self.at, self.send, self.recv = at, send, recv

    def copy(self, src, dst, to):
        return remote(src, dst, self.send.at[to], self.recv.at[self.at.c], (self.at.r, to))

    def wait_from(self, dst, source):
        remote(dst, dst, self.send.at[source], self.recv.at[source], (self.at.r, source)).wait_recv()


class Tree:
    def __init__(self, at, block, sems):
        self.at, self.block = at, block
        self.z_send, self.z_recv, self.y_send, self.y_recv, self.f_send, self.f_recv = sems
        y, zh = lax.div(at.c, 2), lax.rem(at.c, 2)
        self.zhs = (zh, 1 - zh)
        self.ys = (lax.rem(y + 3, 4), lax.rem(y + 1, 4))
        self.y, self.far = y, lax.rem(y + 2, 4)

    def col(self, y, s):
        return 2 * y + self.zhs[s]

    def z_copy(self, s):
        b = self.block(self.col(self.y, s))
        return remote(b, b, self.z_send.at[0], self.z_recv.at[0], (self.at.r, self.col(self.y, 1)))

    def y_copy(self, s, to):
        b = self.block(self.col(self.y, s))
        return remote(b, b, self.y_send.at[s, to], self.y_recv.at[s, 1 - to], (self.at.r, self.col(self.ys[to], 0)))

    def y_wait(self, s, came):
        b = self.block(self.col(self.ys[came], s))
        remote(b, b, self.y_send.at[s, came], self.y_recv.at[s, came], (self.at.r, self.col(self.ys[came], 0))).wait_recv()

    def f_copy(self, s, came):
        b = self.block(self.col(self.ys[came], s), came)
        return remote(b, b, self.f_send.at[s, came], self.f_recv.at[s, came], (self.at.r, self.col(self.ys[1 - came], 0)))

    def f_wait(self, s, came):
        b = self.block(self.col(self.far, s), came)
        remote(b, b, self.f_send.at[s, came], self.f_recv.at[s, came], (self.at.r, self.col(self.ys[came], 0))).wait_recv()

    def stage_own(self):
        self.z_copy(0).start()
        self.y_copy(0, LEFT).start()
        self.y_copy(0, RIGHT).start()

    def stage_partner(self):
        self.z_copy(1).wait_recv()
        self.y_copy(1, LEFT).start()
        self.y_copy(1, RIGHT).start()

    def stage_forward(self, s):
        for came in (LEFT, RIGHT):
            self.y_wait(s, came)
            self.f_copy(s, came).start()

    def stage_far(self, s):
        for came in (LEFT, RIGHT):
            self.f_wait(s, came)

    def drain(self):
        self.z_copy(0).wait_send()
        for s in (0, 1):
            for to in (LEFT, RIGHT):
                self.y_copy(s, to).wait_send()
                self.f_copy(s, to).wait_send()


def panel_kernel(rv_hbm, ru_hbm, cu_hbm, cv_hbm, d_hbm, u_hbm, v_hbm, s_ref, w_ref, t_ref, gram_ref, cores_ref, rs_hbm, us_hbm, vs_hbm, cs_hbm,
                 vblk, vsp, rbuf, rsp, dbuf, dsp, zpart, zsend, zt, zsp, cub, cvb, csp, xsp, ubuf, vbuf, usp, wsp, tts, ttr, uu_s, p1_s, p2_s, ru_s,
                 v_send, v_recv, p_send, p_recv, rz_send, rz_recv, ry_send, ry_recv, rf_send, rf_recv,
                 qz_send, qz_recv, qy_send, qy_recv, qf_send, qf_recv,
                 t_send, t_recv, z_send, z_recv, x_send, x_recv, f_send, f_recv, d_send, d_recv, own_sem, in_sem, out_sem, uv_sem, save_sem):
    cols, part, k = vblk.shape
    tiles = ubuf.shape[0]
    rows = cols * part
    at = Links(cols)
    sems = (t_send, t_recv, z_send, z_recv, x_send, x_recv, f_send, f_recv, d_send, d_recv, own_sem)
    cv = Spread(at, cv_hbm, cvb, sems, 0)
    cu = Spread(at, cu_hbm, cub, sems, 1)
    vg, pg = Group(at, v_send, v_recv), Group(at, p_send, p_recv)

    def span(b):
        return pl.ds(pl.multiple_of(b * part, part), part)

    def rblock(b, half=None):
        if half is None:
            return rbuf.at[span(b), :]
        size = part // 2
        return rbuf.at[pl.ds(pl.multiple_of(b * part + half * size, size), size), :]

    def zblock(b, half=None):
        if half is None:
            return zt.at[b]
        size = k // 2
        return zt.at[b, size * half : size * (half + 1), :]

    rg = Tree(at, rblock, (rz_send, rz_recv, ry_send, ry_recv, rf_send, rf_recv))
    qg = Tree(at, zblock, (qz_send, qz_recv, qy_send, qy_recv, qf_send, qf_recv))

    def others(do, keep=None):
        for step in range(1, cols):
            b = lax.rem(at.c + step, cols)
            if keep is None:
                do(b)
            else:

                @pl.when(keep(b))
                def _(b=b):
                    do(b)

    later, earlier = (lambda b: b > at.c), (lambda b: b < at.c)
    load_d = pltpu.make_async_copy(d_hbm, dbuf, in_sem.at[0])
    load_v = pltpu.make_async_copy(rv_hbm.at[0], vblk.at[at.c], in_sem.at[1])
    load_r = pltpu.make_async_copy(ru_hbm.at[0], rblock(at.c), in_sem.at[2])

    def load_tile(t, which):
        src, dst = ((u_hbm, ubuf), (v_hbm, vbuf))[which]
        return pltpu.make_async_copy(src.at[t], dst.at[t], uv_sem.at[which, t])

    def save(n, t):
        src, dst = ((usp, us_hbm), (wsp, vs_hbm), (csp, cs_hbm))[n]
        return pltpu.make_async_copy(src.at[t], dst.at[t], save_sem.at[n, t])

    load_d.start()
    load_v.start()
    load_r.start()

    def split_d(b, carry):
        d = dbuf[:, span(b)]
        hi = d.astype(bf16)
        dsp[0, :, span(b)] = hi
        dsp[1, :, span(b)] = (d - hi.astype(f32)).astype(bf16)
        return carry

    def prepare():
        for b in range(cols):

            @pl.when(b > at.c)
            def _(b=b):
                vsp[part * b : part * (b + 1), :] = jnp.zeros((part, 2 * k), bf16)

        load_v.wait()
        vsp[span(at.c), :] = halves(vblk[at.c])
        load_d.wait()
        lax.fori_loop(0, cols, split_d, 0)

    greet(at, prepare)
    others(lambda b: vg.copy(rv_hbm.at[0], vblk.at[at.c], b).start(), later)
    cv.transpose_start()
    cu.transpose_start()
    for t in range(tiles):
        load_tile(t, 0).start()
        load_tile(t, 1).start()

    def split_s(b, carry):
        tts[:, span(b)] = halves(s_ref[span(b), :]).astype(f32).T.astype(bf16)
        return carry

    lax.fori_loop(0, cols, split_s, 0)

    def split_into(dst, src):
        def body(b, carry):
            dst[span(b), :] = halves(src[span(b), :])
            return carry

        lax.fori_loop(0, cols, body, 0)

    def split_all(dst, src):
        def body(b, carry):
            for t in range(tiles):
                dst[t, span(b), :] = halves(src[t, span(b), :])
            return carry

        lax.fori_loop(0, cols, body, 0)

    def use_pair(core):
        def body(b, carry):
            for i in range(2):
                csp[2 * core + i, span(b), :] = halves(cub[2 * core + i, span(b), :])
            return carry

        lax.fori_loop(0, cols, body, 0)
        for i in range(2):
            save(2, 2 * core + i).start()
        for i in range(2):
            p2_s[2 * core + i] = fold4(dotb(tts[...], csp[2 * core + i]))

    def tile_products(t):
        load_tile(t, 0).wait()
        load_tile(t, 1).wait()
        split_into(usp.at[t], ubuf.at[t])
        split_into(wsp.at[t], vbuf.at[t])
        save(0, t).start()
        save(1, t).start()
        uu_s[t] = fold4(dotb(usp[t], usp[t], 0, 0))
        p1_s[t] = fold4(dotb(tts[...], wsp[t]))

    cv.stage_own()
    cu.stage_own()

    def arrived(b, carry):
        vg.wait_from(vblk.at[b], b)
        vsp[span(b), :] = halves(vblk[b])
        return carry

    lax.fori_loop(0, at.c, arrived, 0)
    q = dotb(dsp[0], vsp[...]) + dotb(dsp[1], vsp[...])
    yt = halves(q[:, :k] + q[:, k:]).astype(f32).T.astype(bf16)
    for b in range(cols):
        q = dotb(yt, dsp[0, :, part * b : part * (b + 1)]) + dotb(yt, dsp[1, :, part * b : part * (b + 1)])
        zsend[b] = q[:k] + q[k:]
    others(lambda b: pg.copy(zsend.at[b], zpart.at[at.c], b).start(), earlier)
    cv.stage_partner()
    cu.stage_partner()
    load_r.wait()
    rg.stage_own()
    tile_products(0)
    zt[at.c] = zsend[at.c]

    def gather(n, carry):
        b = cols - 1 - n
        pg.wait_from(zpart.at[b], b)
        zt[at.c] = zt[at.c] + zpart[b]
        return carry

    lax.fori_loop(0, cols - 1 - at.c, gather, 0)
    qg.stage_own()
    cv.stage_forward(0)
    cv.stage_forward(1)
    rg.stage_partner()
    tile_products(1)
    qg.stage_partner()
    qg.stage_forward(0)
    cu.stage_forward(0)
    rg.stage_forward(0)
    tile_products(2)
    qg.stage_forward(1)
    rg.stage_forward(1)
    cv.stage_far(0)
    cv.stage_far(1)
    cu.stage_forward(1)
    tile_products(3)
    rg.stage_far(0)
    rg.stage_far(1)
    def split_r(b, carry):
        h = halves(rbuf[span(b), :])
        rsp[span(b), :] = h
        ttr[:, span(b)] = h.astype(f32).T.astype(bf16)
        return carry

    lax.fori_loop(0, cols, split_r, 0)
    out_r = pltpu.make_async_copy(rsp, rs_hbm, out_sem.at[0])
    out_r.start()
    rr = fold4(dotb(ttr[...], rsp[...]))
    for t in range(tiles):
        ru_s[t] = fold4(dotb(ttr[...], usp[t]))
    cv.stage_other_core()
    cu.stage_far(0)
    cu.stage_far(1)
    split_all(xsp, cvb)
    qg.stage_far(0)
    qg.stage_far(1)
    for b in range(cols):
        z = zt[b]
        hi = z.astype(bf16)
        zsp[:k, part * b : part * (b + 1)] = hi
        zsp[k:, part * b : part * (b + 1)] = (z - hi.astype(f32)).astype(bf16)
    for t in range(tiles):
        cores_ref[t] = fold4(dotb(zsp[...], xsp[t]))
    use_pair(at.core)
    cu.stage_other_core()
    use_pair(1 - at.core)
    ws = []
    for t in range(tiles):
        w2 = -dot(cores_ref[t], p2_s[t], 1, 1)
        ws.append(jnp.concatenate([p1_s[t].T, w2], axis=0))
        w_ref[t] = ws[t]
    tws = []
    for t in range(tiles):
        ru = ru_s[t]
        g = jnp.concatenate([jnp.concatenate([uu_s[t], ru.T], axis=1), jnp.concatenate([ru, rr], axis=1)], axis=0)
        tws.append(dot(g, ws[t]))
        t_ref[t] = tws[t]
    for t in range(tiles):
        gram_ref[t] = dot(ws[t], tws[t], 0, 0)

    others(lambda b: vg.copy(rv_hbm.at[0], vblk.at[at.c], b).wait_send(), later)
    others(lambda b: pg.copy(zsend.at[b], zpart.at[at.c], b).wait_send(), earlier)
    rg.drain()
    qg.drain()
    cv.drain()
    cu.drain()
    out_r.wait()
    for t in range(tiles):
        for n in range(3):
            save(n, t).wait()


def spread_panels(row_v, row_u, col_u, col_v, diag, tile_u, tile_v, sketch):
    cols = lax.axis_size("col")
    tiles = tile_u.shape[0]
    part, k = row_v.shape[1:]
    rows = cols * part
    vm = pl.BlockSpec(memory_space=pltpu.VMEM)
    hbm = pl.BlockSpec(memory_space=pltpu.HBM)
    dma = pltpu.SemaphoreType.DMA
    return pl.pallas_call(
        panel_kernel,
        name="spread_panels",
        out_shape=(
            jax.ShapeDtypeStruct((tiles, 2 * k, k), f32),
            jax.ShapeDtypeStruct((tiles, 2 * k, k), f32),
            jax.ShapeDtypeStruct((tiles, k, k), f32),
            jax.ShapeDtypeStruct((tiles, k, k), f32),
            jax.ShapeDtypeStruct((rows, 2 * k), bf16),
            jax.ShapeDtypeStruct((tiles, rows, 2 * k), bf16),
            jax.ShapeDtypeStruct((tiles, rows, 2 * k), bf16),
            jax.ShapeDtypeStruct((tiles, rows, 2 * k), bf16),
        ),
        in_specs=[hbm] * 7 + [vm],
        out_specs=(vm, vm, vm, vm, hbm, hbm, hbm, hbm),
        scratch_shapes=[
            pltpu.VMEM((cols, part, k), f32),
            pltpu.VMEM((rows, 2 * k), bf16),
            pltpu.VMEM((rows, k), f32),
            pltpu.VMEM((rows, 2 * k), bf16),
            pltpu.VMEM((part, rows), f32),
            pltpu.VMEM((2, part, rows), bf16),
            pltpu.VMEM((cols, k, part), f32),
            pltpu.VMEM((cols, k, part), f32),
            pltpu.VMEM((cols, k, part), f32),
            pltpu.VMEM((2 * k, rows), bf16),
            pltpu.VMEM((tiles, rows, k), f32),
            pltpu.VMEM((tiles, rows, k), f32),
            pltpu.VMEM((tiles, rows, 2 * k), bf16),
            pltpu.VMEM((tiles, rows, 2 * k), bf16),
            pltpu.VMEM((tiles, rows, k), f32),
            pltpu.VMEM((tiles, rows, k), f32),
            pltpu.VMEM((tiles, rows, 2 * k), bf16),
            pltpu.VMEM((tiles, rows, 2 * k), bf16),
            pltpu.VMEM((2 * k, rows), bf16),
            pltpu.VMEM((2 * k, rows), bf16),
            pltpu.VMEM((tiles, k, k), f32),
            pltpu.VMEM((tiles, k, k), f32),
            pltpu.VMEM((tiles, k, k), f32),
            pltpu.VMEM((tiles, k, k), f32),
        ]
        + [dma((cols,))] * 4
        + ([dma((1,))] * 2 + [dma((2, 2))] * 4) * 2
        + [dma((2,))] * 4
        + [dma((2, 2, 2))] * 4
        + [dma((2, 10))] * 2
        + [dma((2,)), dma((3,)), dma((1,)), dma((2, tiles)), dma((3, tiles))],
        compiler_params=pltpu.CompilerParams(collective_id=0, has_side_effects=True, vmem_limit_bytes=54 * 2**20),
        cost_estimate=pl.CostEstimate(flops=10**9, bytes_accessed=16 * 2**20, transcendentals=0),
    )(row_v, row_u, col_u, col_v, diag, tile_u, tile_v, sketch)


def body(tile_u, tile_v, row_panel_u, row_panel_v, col_panel_u, col_panel_v, diag_inverse, sketch):
    w, tw, gram, cores, row_u, split_u, split_v, col_u = spread_panels(
        row_panel_v, row_panel_u, col_panel_u, col_panel_v, diag_inverse, tile_u[0], tile_v[0], sketch
    )
    new_u, new_v = recompress(split_u, split_v, row_u, col_u, cores, w, tw, gram)
    return new_u[None], new_v[None]


def solution(mesh):
    in_specs = (
        P("row", "col", None, None),
        P("row", "col", None, None),
        P("row", "col", None),
        P("row", "col", None),
        P("row", "col", None),
        P("row", "col", None),
        P("col", None),
        P(),
    )
    out_specs = (P("row", "col", None, None), P("row", "col", None, None))
    return jax.shard_map(body, mesh=mesh, in_specs=in_specs, out_specs=out_specs, check_vma=False)
```

```python
import math

import jax
import jax.numpy as jnp
from jax import lax
from jax.experimental import pallas as pl
from jax.experimental.pallas import tpu as pltpu
from jax.sharding import PartitionSpec as P

highest = lax.Precision.HIGHEST
f32, bf16 = jnp.float32, jnp.bfloat16
STEP = 2048


def halves(x):
    hi = x.astype(bf16)
    lo = (x - hi.astype(f32)).astype(bf16)
    return jnp.concatenate([hi, lo], axis=1)


def fold4(q):
    k = q.shape[0] // 2
    n = q.shape[1] // 2
    return q[:k, :n] + q[:k, n:] + q[k:, :n] + q[k:, n:]


def doubled(w):
    h = halves(w)
    return jnp.concatenate([h, h], axis=0)


def dot(a, b, ca=1, cb=0, precision=highest):
    return lax.dot_general(a, b, (((ca,), (cb,)), ((), ())), precision=precision, preferred_element_type=f32)


def dotb(a, b, ca=1, cb=0):
    return lax.dot_general(a, b, (((ca,), (cb,)), ((), ())), preferred_element_type=f32)


def dot4(a, b):
    n = b.shape[1]
    q = dotb(halves(a), doubled(b))
    return q[:, :n] + q[:, n:]


def split3(x):
    hi = x.astype(bf16).astype(f32)
    rest = x - hi
    mid = rest.astype(bf16).astype(f32)
    return hi, mid, rest - mid


def outer(a, b):
    ah, am, al = split3(a)
    bh, bm, bl = split3(b)
    left = jnp.concatenate([ah, am, ah, al, ah, am], axis=0).astype(bf16)
    right = jnp.concatenate([bh, bh, bm, bh, bl, bm], axis=0).astype(bf16)
    return dotb(left, right, 0, 0)


def inverse_factors(gram_ref, inv_ref, fac_ref):
    tiles, k, _ = gram_ref.shape
    row = lax.broadcasted_iota(jnp.int32, (tiles, 8, k), 1)
    lane = lax.broadcasted_iota(jnp.int32, (tiles, 8, k), 2)
    for p in range(k // 8):
        lo = 8 * p
        panel = gram_ref[:, lo : lo + 8, :]
        if p == 0:
            own = jnp.zeros((tiles, 8, k), f32)
        else:
            own = inv_ref[:, lo : lo + 8, :]
        own = own + jnp.where(lane == row + lo, 1.0, 0.0)
        cols = [jnp.broadcast_to(panel[:, :, lo + i : lo + i + 1], panel.shape) for i in range(8)]
        scale = jnp.zeros((tiles, 8, k), f32)
        pivot = jnp.zeros((tiles, 8, k), f32)
        for i in range(8):
            piv = jnp.broadcast_to(cols[i][:, i : i + 1, :], panel.shape)
            recip = 1.0 / piv
            scale = jnp.where(row == i, recip, scale)
            if i < 7:
                m = jnp.where(row > i, cols[i] * recip, 0.0)
                for j in range(i + 1, 8):
                    cols[j] = cols[j] - m * cols[j][:, i : i + 1, :]
                panel = panel - m * panel[:, i : i + 1, :]
                own = own - m * own[:, i : i + 1, :]
        fac_ref[:, lo : lo + 8, :] = own * jnp.sqrt(scale)
        if p < k // 8 - 1:
            lower = panel * scale
            for t in range(tiles):
                both = jnp.concatenate([panel[t], own[t]], axis=1)
                upd = outer(lower[t], both)
                gram_ref[t, lo + 8 :, :] = gram_ref[t, lo + 8 :, :] - upd[lo + 8 :, :k]
                if p == 0:
                    inv_ref[t, lo + 8 :, :] = -upd[lo + 8 :, k:]
                else:
                    inv_ref[t, lo + 8 :, :] = inv_ref[t, lo + 8 :, :] - upd[lo + 8 :, k:]


def finish_kernel(u_hbm, v_hbm, r_hbm, c_hbm, cores_hbm, w_hbm, t_hbm, gram_hbm, nu_hbm, nv_hbm,
                  ubuf, vbuf, cbuf, rbuf, uout, vout, cores_ref, w_ref, t_ref, gram_s, inv_s, fac_s, wide_s, in_sem, r_sem, out_sem):
    tiles, rows, k = uout.shape
    step = min(STEP, rows)
    scaling = math.sqrt(rows)

    def load(t, which):
        src, dst = ((u_hbm, ubuf), (v_hbm, vbuf), (c_hbm, cbuf))[which]
        return pltpu.make_async_copy(src.at[t], dst.at[t], in_sem.at[which, t])

    singles = [
        pltpu.make_async_copy(src, dst, r_sem.at[n])
        for n, (src, dst) in enumerate(((gram_hbm, gram_s), (w_hbm, w_ref), (t_hbm, t_ref), (cores_hbm, cores_ref), (r_hbm, rbuf)))
    ]
    for copy in singles:
        copy.start()
    for t in range(tiles):
        for which in range(3):
            load(t, which).start()
    singles[0].wait()
    inverse_factors(gram_s, inv_s, fac_s)

    def store(t, which):
        src, dst = ((uout, nu_hbm), (vout, nv_hbm))[which]
        return pltpu.make_async_copy(src.at[t], dst.at[t], out_sem.at[which, t])

    for copy in singles[1:]:
        copy.wait()
    for t in range(tiles):
        fac = fac_s[t]
        fac_t = fac.T
        x = dot4(w_ref[t], fac_t) * scaling
        y = dot4(t_ref[t], fac_t) * (1.0 / scaling)
        c2 = -dot4(cores_ref[t].T, y[k:])
        for n, part in enumerate((x[:k], x[k:], y[:k], c2)):
            wide_s[t, n] = doubled(part)
    for t in range(tiles):
        for which in range(3):
            load(t, which).wait()

        def finish(n, carry, t=t):
            at = pl.ds(pl.multiple_of(n * step, step), step)
            a = dotb(ubuf[t, at, :], wide_s[t, 0]) + dotb(rbuf[at, :], wide_s[t, 1])
            uout[t, at, :] = a[:, :k] + a[:, k:]
            b = dotb(vbuf[t, at, :], wide_s[t, 2]) + dotb(cbuf[t, at, :], wide_s[t, 3])
            vout[t, at, :] = b[:, :k] + b[:, k:]
            return carry

        lax.fori_loop(0, rows // step, finish, 0)
        store(t, 0).start()
        store(t, 1).start()
    for t in range(tiles):
        store(t, 0).wait()
        store(t, 1).wait()


def recompress(tile_u, tile_v, row_u, col_u, cores, w, tw, gram):
    tiles, rows, k = tile_u.shape[0], tile_u.shape[1], cores.shape[1]
    hbm = pl.BlockSpec(memory_space=pltpu.HBM)
    out = jax.ShapeDtypeStruct((tiles, rows, k), f32)
    return pl.pallas_call(
        finish_kernel,
        name="recompress",
        out_shape=(out, out),
        in_specs=[hbm] * 8,
        out_specs=(hbm, hbm),
        scratch_shapes=[
            pltpu.VMEM((tiles, rows, 2 * k), bf16),
            pltpu.VMEM((tiles, rows, 2 * k), bf16),
            pltpu.VMEM((tiles, rows, 2 * k), bf16),
            pltpu.VMEM((rows, 2 * k), bf16),
            pltpu.VMEM((tiles, rows, k), f32),
            pltpu.VMEM((tiles, rows, k), f32),
            pltpu.VMEM((tiles, k, k), f32),
            pltpu.VMEM((tiles, 2 * k, k), f32),
            pltpu.VMEM((tiles, 2 * k, k), f32),
            pltpu.VMEM((tiles, k, k), f32),
            pltpu.VMEM((tiles, k, k), f32),
            pltpu.VMEM((tiles, k, k), f32),
            pltpu.VMEM((tiles, 4, 2 * k, 2 * k), bf16),
            pltpu.SemaphoreType.DMA((3, tiles)),
            pltpu.SemaphoreType.DMA((5,)),
            pltpu.SemaphoreType.DMA((2, tiles)),
        ],
        compiler_params=pltpu.CompilerParams(vmem_limit_bytes=60 * 2**20),
        cost_estimate=pl.CostEstimate(flops=10**10, bytes_accessed=24 * 2**20, transcendentals=0),
    )(tile_u, tile_v, row_u, col_u, cores, w, tw, gram)


MESH = pl.DeviceIdType.MESH
CENTRE, ACROSS, LEFT, RIGHT = 0, 1, 0, 1


def mix(a, b):
    out = 0
    for bit in (4, 2, 1):
        out = out + bit * lax.rem(lax.div(a, bit) + lax.div(b, bit), 2)
    return out


class Links:
    def __init__(self, cols):
        self.r = lax.axis_index("row")
        self.c = lax.axis_index("col")
        self.cols = cols
        self.core = lax.rem(self.r, 2)
        self.m = lax.div(self.r, 2)
        self.x = lax.rem(self.m, 4)
        self.zl = lax.div(self.m, 4)
        self.turn = 6 * self.core
        self.mixed = mix(mix(self.m, self.c), self.turn)
        self.target = (2 * self.mixed + self.core, self.m)
        self.source = (2 * self.c + self.core, self.mixed)
        self.alone = jnp.logical_and(self.m == self.c, self.c == self.turn)

    def chip(self, zl, x):
        return 4 * zl + x

    def at_chip(self, m):
        return (2 * m + self.core, self.c)


def remote(src, dst, send, recv, device):
    return pltpu.make_async_remote_copy(
        src_ref=src, dst_ref=dst, send_sem=send, recv_sem=recv, device_id=device, device_id_type=MESH
    )


class Spread:
    def __init__(self, at, src, buf, sems, w):
        self.at, self.src, self.buf, self.w = at, src, buf, w
        (self.t_send, self.t_recv, self.z_send, self.z_recv, self.x_send, self.x_recv,
         self.f_send, self.f_recv, self.d_send, self.d_recv, self.own_sem) = sems
        self.rows = src.shape[1]
        self.other = (at.r + 1 - 2 * at.core, at.c)
        xl, xr = lax.rem(at.x + 3, 4), lax.rem(at.x + 1, 4)
        self.xs = (xl, xr)
        self.far = lax.rem(at.x + 2, 4)
        self.zls = (at.zl, 1 - at.zl)

    def block(self, m, core=None, tile=None):
        core = self.at.core if core is None else core
        rows = pl.ds(pl.multiple_of(mix(mix(m, self.at.c), 6 * core) * self.rows, self.rows), self.rows)
        if tile is None:
            return self.buf.at[pl.ds(2 * core, 2), rows, :]
        return self.buf.at[pl.ds(2 * core + tile, 1), rows, :]

    def transpose_copy(self):
        at = self.at
        rows = pl.ds(pl.multiple_of(at.c * self.rows, self.rows), self.rows)
        dst = self.buf.at[pl.ds(2 * at.core, 2), rows, :]
        return remote(self.src, dst, self.t_send.at[self.w], self.t_recv.at[self.w], at.target)

    def transpose_local(self):
        return pltpu.make_async_copy(self.src, self.block(self.at.m), self.own_sem.at[self.w])

    def transpose_start(self):
        @pl.when(jnp.logical_not(self.at.alone))
        def _():
            self.transpose_copy().start()

        @pl.when(self.at.alone)
        def _():
            self.transpose_local().start()

    def transpose_wait(self):
        at = self.at

        @pl.when(jnp.logical_not(at.alone))
        def _():
            own = self.block(at.m)
            remote(own, own, self.t_send.at[self.w], self.t_recv.at[self.w], at.source).wait_recv()

        @pl.when(at.alone)
        def _():
            self.transpose_local().wait()

    def z_copy(self, zl):
        b = self.block(self.at.chip(zl, self.at.x))
        return remote(b, b, self.z_send.at[self.w], self.z_recv.at[self.w], self.at.at_chip(self.at.chip(self.zls[1], self.at.x)))

    def x_copy(self, s, to):
        b = self.block(self.at.chip(self.zls[s], self.at.x))
        return remote(b, b, self.x_send.at[self.w, s, to], self.x_recv.at[self.w, s, 1 - to], self.at.at_chip(self.at.chip(self.at.zl, self.xs[to])))

    def x_wait(self, s, came):
        b = self.block(self.at.chip(self.zls[s], self.xs[came]))
        remote(b, b, self.x_send.at[self.w, s, came], self.x_recv.at[self.w, s, came], self.other).wait_recv()

    def f_copy(self, s, came):
        b = self.block(self.at.chip(self.zls[s], self.xs[came]), tile=came)
        return remote(b, b, self.f_send.at[self.w, s, came], self.f_recv.at[self.w, s, came], self.at.at_chip(self.at.chip(self.at.zl, self.xs[1 - came])))

    def f_wait(self, s, came):
        b = self.block(self.at.chip(self.zls[s], self.far), tile=came)
        remote(b, b, self.f_send.at[self.w, s, came], self.f_recv.at[self.w, s, came], self.other).wait_recv()

    def d_copy(self, n, core=None):
        at = self.at
        core = at.core if core is None else core
        if n < 2:
            b = self.block(at.chip(self.zls[n], at.x), core)
        elif n < 6:
            s, came = divmod(n - 2, 2)
            b = self.block(at.chip(self.zls[s], self.xs[came]), core)
        else:
            s, came = divmod(n - 6, 2)
            b = self.block(at.chip(self.zls[s], self.far), core, came)
        return remote(b, b, self.d_send.at[self.w, n], self.d_recv.at[self.w, n], self.other)

    def stage_own(self):
        self.transpose_wait()
        self.x_copy(0, LEFT).start()
        self.x_copy(0, RIGHT).start()
        self.z_copy(self.zls[0]).start()
        self.d_copy(0).start()

    def stage_partner(self):
        self.z_copy(self.zls[1]).wait_recv()
        self.x_copy(1, LEFT).start()
        self.x_copy(1, RIGHT).start()
        self.d_copy(1).start()

    def stage_forward(self, s):
        for came in (LEFT, RIGHT):
            self.x_wait(s, came)
            self.f_copy(s, came).start()
            self.d_copy(2 + 2 * s + came).start()

    def stage_far(self, s):
        for came in (LEFT, RIGHT):
            self.f_wait(s, came)
            self.d_copy(6 + 2 * s + came).start()

    def stage_other_core(self):
        for n in range(10):
            self.d_copy(n, 1 - self.at.core).wait_recv()

    def drain(self):
        @pl.when(jnp.logical_not(self.at.alone))
        def _():
            self.transpose_copy().wait_send()

        self.z_copy(self.zls[0]).wait_send()
        for s in (0, 1):
            for to in (LEFT, RIGHT):
                self.x_copy(s, to).wait_send()
                self.f_copy(s, to).wait_send()
        for n in range(10):
            self.d_copy(n).wait_send()


def greet(at, before_wait):
    barrier = pltpu.get_barrier_semaphore()

    def hello(device):
        pl.semaphore_signal(barrier, inc=1, device_id=device, device_id_type=MESH)

    for step in range(1, at.cols):
        hello((at.r, lax.rem(at.c + step, at.cols)))
    hello((at.r + 1 - 2 * at.core, at.c))
    hello(at.at_chip(at.chip(1 - at.zl, at.x)))
    hello(at.at_chip(at.chip(at.zl, lax.rem(at.x + 1, 4))))
    hello(at.at_chip(at.chip(at.zl, lax.rem(at.x + 3, 4))))

    @pl.when(jnp.logical_not(at.alone))
    def _():
        hello(at.target)
        hello(at.source)

    before_wait()

    @pl.when(jnp.logical_not(at.alone))
    def _():
        pl.semaphore_wait(barrier, at.cols + 5)

    @pl.when(at.alone)
    def _():
        pl.semaphore_wait(barrier, at.cols + 3)


class Group:
    def __init__(self, at, send, recv):
        self.at, self.send, self.recv = at, send, recv

    def copy(self, src, dst, to):
        return remote(src, dst, self.send.at[to], self.recv.at[self.at.c], (self.at.r, to))

    def wait_from(self, dst, source):
        remote(dst, dst, self.send.at[source], self.recv.at[source], (self.at.r, source)).wait_recv()


class Tree:
    def __init__(self, at, block, sems):
        self.at, self.block = at, block
        self.z_send, self.z_recv, self.y_send, self.y_recv, self.f_send, self.f_recv = sems
        y, zh = lax.div(at.c, 2), lax.rem(at.c, 2)
        self.zhs = (zh, 1 - zh)
        self.ys = (lax.rem(y + 3, 4), lax.rem(y + 1, 4))
        self.y, self.far = y, lax.rem(y + 2, 4)

    def col(self, y, s):
        return 2 * y + self.zhs[s]

    def z_copy(self, s):
        b = self.block(self.col(self.y, s))
        return remote(b, b, self.z_send.at[0], self.z_recv.at[0], (self.at.r, self.col(self.y, 1)))

    def y_copy(self, s, to):
        b = self.block(self.col(self.y, s))
        return remote(b, b, self.y_send.at[s, to], self.y_recv.at[s, 1 - to], (self.at.r, self.col(self.ys[to], 0)))

    def y_wait(self, s, came):
        b = self.block(self.col(self.ys[came], s))
        remote(b, b, self.y_send.at[s, came], self.y_recv.at[s, came], (self.at.r, self.col(self.ys[came], 0))).wait_recv()

    def f_copy(self, s, came):
        b = self.block(self.col(self.ys[came], s), came)
        return remote(b, b, self.f_send.at[s, came], self.f_recv.at[s, came], (self.at.r, self.col(self.ys[1 - came], 0)))

    def f_wait(self, s, came):
        b = self.block(self.col(self.far, s), came)
        remote(b, b, self.f_send.at[s, came], self.f_recv.at[s, came], (self.at.r, self.col(self.ys[came], 0))).wait_recv()

    def stage_own(self):
        self.z_copy(0).start()
        self.y_copy(0, LEFT).start()
        self.y_copy(0, RIGHT).start()

    def stage_partner(self):
        self.z_copy(1).wait_recv()
        self.y_copy(1, LEFT).start()
        self.y_copy(1, RIGHT).start()

    def stage_forward(self, s):
        for came in (LEFT, RIGHT):
            self.y_wait(s, came)
            self.f_copy(s, came).start()

    def stage_far(self, s):
        for came in (LEFT, RIGHT):
            self.f_wait(s, came)

    def drain(self):
        self.z_copy(0).wait_send()
        for s in (0, 1):
            for to in (LEFT, RIGHT):
                self.y_copy(s, to).wait_send()
                self.f_copy(s, to).wait_send()


def panel_kernel(rv_hbm, ru_hbm, cu_hbm, cv_hbm, d_hbm, u_hbm, v_hbm, s_ref, w_ref, t_ref, gram_ref, cores_ref, rs_hbm, us_hbm, vs_hbm, cs_hbm,
                 vblk, vsp, rbuf, rsp, dbuf, dsp, zpart, zsend, zt, zsp, cub, cvb, csp, xsp, ubuf, vbuf, usp, wsp, tts, ttr, uu_s, p1_s, p2_s, ru_s,
                 v_send, v_recv, p_send, p_recv, rz_send, rz_recv, ry_send, ry_recv, rf_send, rf_recv,
                 qz_send, qz_recv, qy_send, qy_recv, qf_send, qf_recv,
                 t_send, t_recv, z_send, z_recv, x_send, x_recv, f_send, f_recv, d_send, d_recv, own_sem, in_sem, out_sem, uv_sem, save_sem):
    cols, part, k = vblk.shape
    tiles = ubuf.shape[0]
    rows = cols * part
    at = Links(cols)
    sems = (t_send, t_recv, z_send, z_recv, x_send, x_recv, f_send, f_recv, d_send, d_recv, own_sem)
    cv = Spread(at, cv_hbm, cvb, sems, 0)
    cu = Spread(at, cu_hbm, cub, sems, 1)
    vg, pg = Group(at, v_send, v_recv), Group(at, p_send, p_recv)

    def span(b):
        return pl.ds(pl.multiple_of(b * part, part), part)

    def rblock(b, half=None):
        if half is None:
            return rbuf.at[span(b), :]
        size = part // 2
        return rbuf.at[pl.ds(pl.multiple_of(b * part + half * size, size), size), :]

    def zblock(b, half=None):
        if half is None:
            return zt.at[b]
        size = k // 2
        return zt.at[b, size * half : size * (half + 1), :]

    rg = Tree(at, rblock, (rz_send, rz_recv, ry_send, ry_recv, rf_send, rf_recv))
    qg = Tree(at, zblock, (qz_send, qz_recv, qy_send, qy_recv, qf_send, qf_recv))

    def others(do, keep=None):
        for step in range(1, cols):
            b = lax.rem(at.c + step, cols)
            if keep is None:
                do(b)
            else:

                @pl.when(keep(b))
                def _(b=b):
                    do(b)

    later, earlier = (lambda b: b > at.c), (lambda b: b < at.c)
    load_d = pltpu.make_async_copy(d_hbm, dbuf, in_sem.at[0])
    load_v = pltpu.make_async_copy(rv_hbm.at[0], vblk.at[at.c], in_sem.at[1])
    load_r = pltpu.make_async_copy(ru_hbm.at[0], rblock(at.c), in_sem.at[2])

    def load_tile(t, which):
        src, dst = ((u_hbm, ubuf), (v_hbm, vbuf))[which]
        return pltpu.make_async_copy(src.at[t], dst.at[t], uv_sem.at[which, t])

    def save(n, t):
        src, dst = ((usp, us_hbm), (wsp, vs_hbm), (csp, cs_hbm))[n]
        return pltpu.make_async_copy(src.at[t], dst.at[t], save_sem.at[n, t])

    load_d.start()
    load_v.start()
    load_r.start()

    def split_d(b, carry):
        d = dbuf[:, span(b)]
        hi = d.astype(bf16)
        dsp[0, :, span(b)] = hi
        dsp[1, :, span(b)] = (d - hi.astype(f32)).astype(bf16)
        return carry

    def prepare():
        for b in range(cols):

            @pl.when(b > at.c)
            def _(b=b):
                vsp[part * b : part * (b + 1), :] = jnp.zeros((part, 2 * k), bf16)

        load_v.wait()
        vsp[span(at.c), :] = halves(vblk[at.c])
        load_d.wait()
        lax.fori_loop(0, cols, split_d, 0)

    greet(at, prepare)
    others(lambda b: vg.copy(rv_hbm.at[0], vblk.at[at.c], b).start(), later)
    cv.transpose_start()
    cu.transpose_start()
    for t in range(tiles):
        load_tile(t, 0).start()
        load_tile(t, 1).start()

    def split_s(b, carry):
        tts[:, span(b)] = halves(s_ref[span(b), :]).astype(f32).T.astype(bf16)
        return carry

    lax.fori_loop(0, cols, split_s, 0)

    def split_into(dst, src):
        def body(b, carry):
            dst[span(b), :] = halves(src[span(b), :])
            return carry

        lax.fori_loop(0, cols, body, 0)

    def split_all(dst, src):
        def body(b, carry):
            for t in range(tiles):
                dst[t, span(b), :] = halves(src[t, span(b), :])
            return carry

        lax.fori_loop(0, cols, body, 0)

    def use_pair(core):
        def body(b, carry):
            for i in range(2):
                csp[2 * core + i, span(b), :] = halves(cub[2 * core + i, span(b), :])
            return carry

        lax.fori_loop(0, cols, body, 0)
        for i in range(2):
            save(2, 2 * core + i).start()
        for i in range(2):
            p2_s[2 * core + i] = fold4(dotb(tts[...], csp[2 * core + i]))

    def tile_products(t):
        load_tile(t, 0).wait()
        load_tile(t, 1).wait()
        split_into(usp.at[t], ubuf.at[t])
        split_into(wsp.at[t], vbuf.at[t])
        save(0, t).start()
        save(1, t).start()
        uu_s[t] = fold4(dotb(usp[t], usp[t], 0, 0))
        p1_s[t] = fold4(dotb(tts[...], wsp[t]))

    cv.stage_own()
    cu.stage_own()

    def arrived(b, carry):
        vg.wait_from(vblk.at[b], b)
        vsp[span(b), :] = halves(vblk[b])
        return carry

    lax.fori_loop(0, at.c, arrived, 0)
    q = dotb(dsp[0], vsp[...]) + dotb(dsp[1], vsp[...])
    yt = halves(q[:, :k] + q[:, k:]).astype(f32).T.astype(bf16)
    for b in range(cols):
        q = dotb(yt, dsp[0, :, part * b : part * (b + 1)]) + dotb(yt, dsp[1, :, part * b : part * (b + 1)])
        zsend[b] = q[:k] + q[k:]
    others(lambda b: pg.copy(zsend.at[b], zpart.at[at.c], b).start(), earlier)
    cv.stage_partner()
    cu.stage_partner()
    load_r.wait()
    rg.stage_own()
    tile_products(0)
    zt[at.c] = zsend[at.c]

    def gather(n, carry):
        b = cols - 1 - n
        pg.wait_from(zpart.at[b], b)
        zt[at.c] = zt[at.c] + zpart[b]
        return carry

    lax.fori_loop(0, cols - 1 - at.c, gather, 0)
    qg.stage_own()
    cv.stage_forward(0)
    cv.stage_forward(1)
    rg.stage_partner()
    tile_products(1)
    qg.stage_partner()
    qg.stage_forward(0)
    cu.stage_forward(0)
    rg.stage_forward(0)
    tile_products(2)
    qg.stage_forward(1)
    rg.stage_forward(1)
    cv.stage_far(0)
    cv.stage_far(1)
    cu.stage_forward(1)
    tile_products(3)
    rg.stage_far(0)
    rg.stage_far(1)
    def split_r(b, carry):
        h = halves(rbuf[span(b), :])
        rsp[span(b), :] = h
        ttr[:, span(b)] = h.astype(f32).T.astype(bf16)
        return carry

    lax.fori_loop(0, cols, split_r, 0)
    out_r = pltpu.make_async_copy(rsp, rs_hbm, out_sem.at[0])
    out_r.start()
    rr = fold4(dotb(ttr[...], rsp[...]))
    for t in range(tiles):
        ru_s[t] = fold4(dotb(ttr[...], usp[t]))
    cv.stage_other_core()
    cu.stage_far(0)
    cu.stage_far(1)
    split_all(xsp, cvb)
    qg.stage_far(0)
    qg.stage_far(1)
    for b in range(cols):
        z = zt[b]
        hi = z.astype(bf16)
        zsp[:k, part * b : part * (b + 1)] = hi
        zsp[k:, part * b : part * (b + 1)] = (z - hi.astype(f32)).astype(bf16)
    for t in range(tiles):
        cores_ref[t] = fold4(dotb(zsp[...], xsp[t]))
    use_pair(at.core)
    cu.stage_other_core()
    use_pair(1 - at.core)
    ws = []
    for t in range(tiles):
        w2 = -dot4(cores_ref[t], p2_s[t].T)
        ws.append(jnp.concatenate([p1_s[t].T, w2], axis=0))
        w_ref[t] = ws[t]
    tws = []
    for t in range(tiles):
        ru = ru_s[t]
        g = jnp.concatenate([jnp.concatenate([uu_s[t], ru.T], axis=1), jnp.concatenate([ru, rr], axis=1)], axis=0)
        tws.append(dot4(g, ws[t]))
        t_ref[t] = tws[t]
    for t in range(tiles):
        gram_ref[t] = dot4(ws[t].T, tws[t])

    others(lambda b: vg.copy(rv_hbm.at[0], vblk.at[at.c], b).wait_send(), later)
    others(lambda b: pg.copy(zsend.at[b], zpart.at[at.c], b).wait_send(), earlier)
    rg.drain()
    qg.drain()
    cv.drain()
    cu.drain()
    out_r.wait()
    for t in range(tiles):
        for n in range(3):
            save(n, t).wait()


def spread_panels(row_v, row_u, col_u, col_v, diag, tile_u, tile_v, sketch):
    cols = lax.axis_size("col")
    tiles = tile_u.shape[0]
    part, k = row_v.shape[1:]
    rows = cols * part
    vm = pl.BlockSpec(memory_space=pltpu.VMEM)
    hbm = pl.BlockSpec(memory_space=pltpu.HBM)
    dma = pltpu.SemaphoreType.DMA
    return pl.pallas_call(
        panel_kernel,
        name="spread_panels",
        out_shape=(
            jax.ShapeDtypeStruct((tiles, 2 * k, k), f32),
            jax.ShapeDtypeStruct((tiles, 2 * k, k), f32),
            jax.ShapeDtypeStruct((tiles, k, k), f32),
            jax.ShapeDtypeStruct((tiles, k, k), f32),
            jax.ShapeDtypeStruct((rows, 2 * k), bf16),
            jax.ShapeDtypeStruct((tiles, rows, 2 * k), bf16),
            jax.ShapeDtypeStruct((tiles, rows, 2 * k), bf16),
            jax.ShapeDtypeStruct((tiles, rows, 2 * k), bf16),
        ),
        in_specs=[hbm] * 7 + [vm],
        out_specs=(vm, vm, vm, vm, hbm, hbm, hbm, hbm),
        scratch_shapes=[
            pltpu.VMEM((cols, part, k), f32),
            pltpu.VMEM((rows, 2 * k), bf16),
            pltpu.VMEM((rows, k), f32),
            pltpu.VMEM((rows, 2 * k), bf16),
            pltpu.VMEM((part, rows), f32),
            pltpu.VMEM((2, part, rows), bf16),
            pltpu.VMEM((cols, k, part), f32),
            pltpu.VMEM((cols, k, part), f32),
            pltpu.VMEM((cols, k, part), f32),
            pltpu.VMEM((2 * k, rows), bf16),
            pltpu.VMEM((tiles, rows, k), f32),
            pltpu.VMEM((tiles, rows, k), f32),
            pltpu.VMEM((tiles, rows, 2 * k), bf16),
            pltpu.VMEM((tiles, rows, 2 * k), bf16),
            pltpu.VMEM((tiles, rows, k), f32),
            pltpu.VMEM((tiles, rows, k), f32),
            pltpu.VMEM((tiles, rows, 2 * k), bf16),
            pltpu.VMEM((tiles, rows, 2 * k), bf16),
            pltpu.VMEM((2 * k, rows), bf16),
            pltpu.VMEM((2 * k, rows), bf16),
            pltpu.VMEM((tiles, k, k), f32),
            pltpu.VMEM((tiles, k, k), f32),
            pltpu.VMEM((tiles, k, k), f32),
            pltpu.VMEM((tiles, k, k), f32),
        ]
        + [dma((cols,))] * 4
        + ([dma((1,))] * 2 + [dma((2, 2))] * 4) * 2
        + [dma((2,))] * 4
        + [dma((2, 2, 2))] * 4
        + [dma((2, 10))] * 2
        + [dma((2,)), dma((3,)), dma((1,)), dma((2, tiles)), dma((3, tiles))],
        compiler_params=pltpu.CompilerParams(collective_id=0, has_side_effects=True, vmem_limit_bytes=54 * 2**20),
        cost_estimate=pl.CostEstimate(flops=10**9, bytes_accessed=16 * 2**20, transcendentals=0),
    )(row_v, row_u, col_u, col_v, diag, tile_u, tile_v, sketch)


def body(tile_u, tile_v, row_panel_u, row_panel_v, col_panel_u, col_panel_v, diag_inverse, sketch):
    w, tw, gram, cores, row_u, split_u, split_v, col_u = spread_panels(
        row_panel_v, row_panel_u, col_panel_u, col_panel_v, diag_inverse, tile_u[0], tile_v[0], sketch
    )
    new_u, new_v = recompress(split_u, split_v, row_u, col_u, cores, w, tw, gram)
    return new_u[None], new_v[None]


def solution(mesh):
    in_specs = (
        P("row", "col", None, None),
        P("row", "col", None, None),
        P("row", "col", None),
        P("row", "col", None),
        P("row", "col", None),
        P("row", "col", None),
        P("col", None),
        P(),
    )
    out_specs = (P("row", "col", None, None), P("row", "col", None, None))
    return jax.shard_map(body, mesh=mesh, in_specs=in_specs, out_specs=out_specs, check_vma=False)
```
